256 devices in a mesh: resp: 8 (over y, x_hi), expert: 16 (over z, x_lo), group: 2 (over core).
Axes of the slice: x: 4 (x_hi: 2, x_lo: 2; x = x_hi * 2 + x_lo), y: 4, z: 8, core: 2. Of those that a mesh axis runs over, the one named last changes fastest.
Arguments:
- tokens: bfloat16 [32768, 4096], P(('group', 'resp', 'expert')), parts along dimension 0, may hold values from -6 to 6
- cotangent: bfloat16 [32768, 4096], P(('group', 'resp', 'expert')), parts along dimension 0, may hold values from -6 to 6
- expert_ids: int32 [32768, 1], P(('group', 'resp', 'expert')), parts along dimension 0, may hold values from 0 to 15; in each aligned block of 128 rows (0 to 127, 128 to 255, ...) at most 9 rows name the same one
- gate_weights: float32 [32768, 1], P(('group', 'resp', 'expert')), parts along dimension 0, may hold values from 0.05 to 1
- gate_proj: bfloat16 [16, 1536, 4096], P('expert', 'resp'), may hold values from -0.09375 to 0.09375
- up_proj: bfloat16 [16, 1536, 4096], P('expert', 'resp'), may hold values from -0.09375 to 0.09375
- down_proj: bfloat16 [16, 1536, 4096], P('expert', 'resp'), may hold values from -0.15625 to 0.15625
Outputs:
- token_grad: bfloat16 [32768, 4096], P(('group', 'resp', 'expert')), parts along dimension 0
- gate_proj_grad: bfloat16 [32, 1536, 4096], P(('group', 'expert'), 'resp'), parts along dimension 0
- up_proj_grad: bfloat16 [32, 1536, 4096], P(('group', 'expert'), 'resp'), parts along dimension 0
- down_proj_grad: bfloat16 [32, 1536, 4096], P(('group', 'expert'), 'resp'), parts along dimension 0
The draws below stay inside these ranges and needn't reach their ends.
There are 2 independent parts, one for each index of `group`. The reference program is written for one: setup_inputs(seed, part) draws one part's arguments, and reference() takes and returns one part's arrays. A program takes and returns all parts, laid end to end along the dimension named above; an argument that names none is the same for every part. Nothing has to cross between parts.
Inputs may be any that keep to these rules, and one draw needn't show every extreme that they name: `expert_ids`: among the 128 tokens of one device no expert is named more than 9 times, and in every draw some device names some expert exactly 9 times.
All inputs are finite; a program needn't handle non-finite values.
Results may differ from the reference program's by a relative error of at most 0.017.
Values may be sent and summed in bfloat16 or wider, within the bound.
A program may use at most 192 MiB of HBM per device.

```python
import math
import jax
import jax.numpy as jnp
import numpy as np
from jax import lax

D = 4096
FF = 1536
TOK_DEV = 128
EXPERTS = 16
CAP = 9
TOKENS = 16384
N_RESP = 8
N_EXPERT = 16


def steps_of(key, shape, cuts, low, high):
    loudness, own = 1.0, jax.random.fold_in(key, 6)
    for position, shards_of in cuts:
        heights = jnp.exp(jax.random.uniform(jax.random.fold_in(own, position), (shards_of,), jnp.float32, low / len(cuts), high / len(cuts)))
        loudness = loudness * jnp.repeat(heights, shape[position] // shards_of).reshape([-1 if axis == position else 1 for axis in range(len(shape))])
    return loudness


def deal_out(stream_key, own, number, rows, amount, top, bound, skew):
    ranking = jax.random.permutation(stream_key, amount)
    crowded, usual = load_shares(amount, rows * top, bound, skew, True), load_shares(amount, rows * top, bound, skew, False)
    places = jnp.arange(amount)

    def named(tallies, rotation):
        used = int((tallies > 0).sum())
        fixed = max(1, used // 4)
        passed = fixed + (places - fixed + rotation * (used - fixed)) % max(1, amount - fixed)
        return jnp.zeros((amount,), jnp.int32).at[ranking[jnp.where(places < fixed, places, passed)]].set(jnp.asarray(tallies, jnp.int32))

    tallies = jnp.where(number % 4 == 0, named(crowded, number // 4), named(usual, number - number // 4 - 1))
    mixed = jax.random.permutation(jax.random.fold_in(own, 3), amount)
    giver, sink = mixed[0:amount // 2 * 2:2], mixed[1:amount // 2 * 2:2]
    slack = jnp.minimum(tallies[giver] - 1, bound - tallies[sink]) // 2
    slack = jnp.where((giver == ranking[0]) | (sink == ranking[0]) | (tallies[sink] == 0), 0, jnp.maximum(slack, 0))
    passed = jax.random.randint(jax.random.fold_in(own, 4), (amount // 2,), 0, 1 << 20) % (slack + 1)
    tallies = tallies.at[giver].add(-passed).at[sink].add(passed)
    items = jnp.searchsorted(jnp.cumsum(tallies), jnp.arange(rows * top), side="right").astype(jnp.int32)
    listing = items.reshape(top, rows).T
    listing = listing[jax.random.permutation(jax.random.fold_in(own, 1), rows)]
    rotation = jax.random.randint(jax.random.fold_in(own, 2), (rows, 1), 0, top)
    return jnp.take_along_axis(listing, (jnp.arange(top)[None, :] + rotation) % top, axis=1)


def load_shares(number_of, total, most, lean, full):
    loads = [(1 << 20) // math.isqrt(standing ** lean) + 1 for standing in range(1, number_of + 1)]
    largest = most if full else min(most, max(-(-total // number_of), total * loads[0] // sum(loads)))
    least = 1 if total - largest >= number_of - 1 else 0
    given, rest = [largest] + [least] * (number_of - 1), total - largest - least * (number_of - 1)
    while rest > 0:
        movable = [i for i in range(1, number_of) if given[i] < largest] or [i for i in range(1, number_of) if given[i] < most]
        pool, left = sum([loads[i] for i in movable]), rest
        for i in movable:
            extra = min(most - given[i], max(1, left * loads[i] // pool), rest)
            given[i] = given[i] + extra
            rest = rest - extra
    return np.array(given)


def bell_draw(rng, shape, width, bound, shards=(), held_as=jnp.bfloat16):
    values = jax.random.normal(rng, shape, jnp.float32) * width
    if len(shards) > 0:
        values = steps_of(rng, shape, shards, -0.22, 0.18) * values
    return jnp.clip(values, min=-bound, max=bound).astype(held_as)


def setup_inputs(seed: int = 0, part: int = 0) -> dict:
    streams_of = jax.random.split(jax.random.key(seed), 8)
    part_splits = jax.random.split(jax.random.fold_in(streams_of[7], part), 8)
    tokens = bell_draw(part_splits[0], (TOKENS, D), 1.0, 6.0, ((0, 128),))
    cotangent = bell_draw(part_splits[1], (TOKENS, D), 1.0, 6.0, ((0, 128),))
    expert_ids_keys = jax.random.split(jax.random.fold_in(part_splits[2], 1), TOKENS // TOK_DEV)
    expert_ids_turns = jax.random.permutation(jax.random.fold_in(part_splits[2], 3), TOKENS // TOK_DEV)
    expert_ids = jax.vmap(lambda own, number: deal_out(jax.random.fold_in(part_splits[2], 2), own, number, TOK_DEV, EXPERTS, 1, CAP, 2))(expert_ids_keys, expert_ids_turns).reshape((TOKENS, 1))
    gate_weights = jnp.clip(jnp.exp(math.log(1.0) - 2.9957323 * jax.random.uniform(part_splits[3], (TOKENS, 1), jnp.float32) ** steps_of(part_splits[3], (TOKENS, 1), ((0, 128),), -0.2, 0.2)), 0.05, 1.0)
    gate_proj = bell_draw(streams_of[4], (EXPERTS, FF, D), D ** -0.5, 0.09375, ((0, 16), (1, 8)))
    up_proj = bell_draw(streams_of[5], (EXPERTS, FF, D), D ** -0.5, 0.09375, ((0, 16), (1, 8)))
    down_proj = bell_draw(streams_of[6], (EXPERTS, FF, D), FF ** -0.5, 0.15625, ((0, 16), (1, 8)))
    return dict(tokens=tokens, cotangent=cotangent, expert_ids=expert_ids, gate_weights=gate_weights, gate_proj=gate_proj, up_proj=up_proj, down_proj=down_proj)


def expert_pass(x_rows, g_rows, w_gate, w_up, w_down):
    gate_pre = jnp.dot(x_rows, w_gate.T, preferred_element_type=jnp.float32)
    up_pre = jnp.dot(x_rows, w_up.T, preferred_element_type=jnp.float32)
    sigmoid_a = jax.nn.sigmoid(gate_pre)
    activated = gate_pre * sigmoid_a
    hidden = (activated * up_pre).astype(jnp.bfloat16)
    hidden_grad = jnp.dot(g_rows, w_down.T, preferred_element_type=jnp.float32)
    slope = sigmoid_a * (1.0 + gate_pre * (1.0 - sigmoid_a))
    gate_grad = (hidden_grad * up_pre * slope).astype(jnp.bfloat16)
    up_grad = (hidden_grad * activated).astype(jnp.bfloat16)
    down_total = jnp.dot(hidden.T, g_rows, preferred_element_type=jnp.float32).astype(jnp.bfloat16)
    gate_total = jnp.dot(gate_grad.T, x_rows, preferred_element_type=jnp.float32).astype(jnp.bfloat16)
    up_total = jnp.dot(up_grad.T, x_rows, preferred_element_type=jnp.float32).astype(jnp.bfloat16)
    return gate_grad, up_grad, gate_total, up_total, down_total


def reference(tokens, cotangent, expert_ids, gate_weights, gate_proj, up_proj, down_proj):
    token_count = tokens.shape[0]
    model_width = tokens.shape[1]
    hidden_units = gate_proj.shape[1]
    block_units = hidden_units // N_RESP
    chosen = expert_ids[:, 0].astype(jnp.int32)
    scaled = (gate_weights * cotangent.astype(jnp.float32)).astype(jnp.bfloat16)
    padded_x = jnp.concatenate([tokens, jnp.zeros((1, model_width), tokens.dtype)], axis=0)
    padded_g = jnp.concatenate([scaled, jnp.zeros((1, model_width), scaled.dtype)], axis=0)
    slot_count = N_RESP * N_EXPERT * CAP

    def one_expert(expert_index):
        picked = jnp.nonzero(chosen == expert_index, size=slot_count, fill_value=token_count)[0].astype(jnp.int32)
        x_rows = padded_x[picked]
        g_rows = padded_g[picked]
        w_gate = gate_proj[expert_index]
        w_up = up_proj[expert_index]
        w_down = down_proj[expert_index]
        gate_grad, up_grad, gate_total, up_total, down_total = expert_pass(x_rows, g_rows, w_gate, w_up, w_down)
        gate_blocks = gate_grad.astype(jnp.float32).reshape(slot_count, N_RESP, block_units)
        up_blocks = up_grad.astype(jnp.float32).reshape(slot_count, N_RESP, block_units)
        wg_blocks = w_gate.astype(jnp.float32).reshape(N_RESP, block_units, model_width)
        wu_blocks = w_up.astype(jnp.float32).reshape(N_RESP, block_units, model_width)
        partial_value = jnp.einsum("rsf,sfd->rsd", gate_blocks, wg_blocks) + jnp.einsum("rsf,sfd->rsd", up_blocks, wu_blocks)
        partial_value = partial_value.astype(jnp.bfloat16).astype(jnp.float32)
        token_part = jnp.sum(partial_value, axis=1).astype(jnp.bfloat16)
        return picked, token_part, gate_total, up_total, down_total

    picked, parts, gate_all, up_all, down_all = lax.map(one_expert, jnp.arange(EXPERTS, dtype=jnp.int32))
    token_grad = jnp.zeros((token_count + 1, model_width), jnp.bfloat16)
    token_grad = token_grad.at[picked.reshape(-1)].set(parts.reshape(-1, model_width))[:token_count]
    return token_grad, gate_all, up_all, down_all
```

```python
import jax
import jax.numpy as jnp
from jax import lax
from jax.experimental import pallas as pl
from jax.experimental.pallas import tpu as pltpu
from jax.sharding import PartitionSpec as P

MESH = pl.DeviceIdType.MESH
BF16 = jnp.bfloat16
F32 = jnp.float32

TOK = 128
D = 4096
NE = 16
CAP = 9
BLK = NE * CAP
FB = 192
ROWS = 4 * BLK
CH = 2048
LANES = 128
SLAB = CH // LANES
PACK = BLK * SLAB
TC = 512
NT = D // TC
PER = CH // TC


def nt_dot(a, b):
    return lax.dot_general(a, b, (((1,), (1,)), ((), ())), preferred_element_type=F32)


def nn_dot(a, b):
    return jnp.dot(a, b, preferred_element_type=F32)


def loop(n, body, first=0):
    def step(i, carry):
        body(i)
        return carry

    lax.fori_loop(first, n, step, 0)


def kernel(
    tok_hbm, cot_hbm, ids_ref, gw_ref, wg_hbm, wu_hbm, wd_hbm,
    tg_hbm, og_hbm, ou_hbm, od_hbm,
    tok, cot, pt, perm, wgu, wd, send, recv, stage, xa, ga,
    pre, hg, gu, hid, dt, tx, rtx, ty, rty, dsend, drecv, back, tg,
    load_sem, w_ssem, w_rsem, a_ssem, a_rsem, g_ssem, g_rsem,
    x_ssem, x_rsem, y_ssem, y_rsem, d_ssem, d_rsem, b_ssem, b_rsem,
    out_sem, tok_sem,
):
    resp = lax.axis_index("resp")
    me = lax.axis_index("expert")
    core = lax.axis_index("group")
    y = resp // 2
    x_hi = resp % 2
    side = (y + core) % 2
    x_peer = {"resp": y * 2 + (1 - x_hi)}
    y_peer = {"resp": ((y + 1 + 2 * side) % 4) * 2 + x_hi}
    w_peer = {"resp": ((y + 3 + 2 * side) % 4) * 2 + x_hi}

    def remote(src, dst, ssem, rsem, to):
        return pltpu.make_async_remote_copy(
            src_ref=src, dst_ref=dst, send_sem=ssem, recv_sem=rsem, device_id=to, device_id_type=MESH
        )

    loads = [
        pltpu.make_async_copy(tok_hbm, tok, load_sem.at[0]),
        pltpu.make_async_copy(cot_hbm, cot, load_sem.at[1]),
        pltpu.make_async_copy(wg_hbm.at[0], wgu.at[pl.ds(0, FB)], load_sem.at[2]),
        pltpu.make_async_copy(wu_hbm.at[0], wgu.at[pl.ds(2 * FB, FB)], load_sem.at[3]),
        pltpu.make_async_copy(wd_hbm.at[0], wd.at[pl.ds(0, FB)], load_sem.at[4]),
    ]
    for c in loads:
        c.start()

    barrier = pltpu.get_barrier_semaphore()
    for peer in (x_peer, y_peer, w_peer):
        pl.semaphore_signal(barrier, inc=1, device_id=peer, device_id_type=MESH)

    def greet(d):
        pl.semaphore_signal(barrier, inc=1, device_id={"expert": (me + d) % NE}, device_id_type=MESH)

    loop(NE, greet, 1)
    pl.semaphore_wait(barrier, NE + 2)

    w_copies = [
        remote(wg_hbm.at[0], wgu.at[pl.ds(FB, FB)], w_ssem.at[0], w_rsem.at[0], w_peer),
        remote(wu_hbm.at[0], wgu.at[pl.ds(3 * FB, FB)], w_ssem.at[1], w_rsem.at[1], w_peer),
        remote(wd_hbm.at[0], wd.at[pl.ds(FB, FB)], w_ssem.at[2], w_rsem.at[2], w_peer),
    ]
    for c in w_copies:
        c.start()

    ids = ids_ref[...]
    lane = lax.broadcasted_iota(jnp.int32, (TOK, LANES), 1)
    row = lax.broadcasted_iota(jnp.int32, (TOK, LANES), 0)
    onehot = jnp.where(ids == lane, 1.0, 0.0).astype(F32)
    lower = jnp.where(row > lane, 1.0, 0.0).astype(BF16)
    rank = jnp.sum(nn_dot(lower, onehot.astype(BF16)) * onehot, axis=1, keepdims=True)
    target = ids * CAP + rank.astype(jnp.int32)
    slot = lax.broadcasted_iota(jnp.int32, (TOK, 2 * LANES), 1)
    chosen = jnp.where(slot == target, 1.0, 0.0).astype(F32)
    pt[...] = chosen.astype(BF16)
    perm[...] = chosen.T.astype(BF16)

    def a2a(buf_s, buf_r, ssem, rsem, c, other, mine):
        return remote(
            buf_s.at[c, pl.ds(pl.multiple_of(other * BLK, 16), BLK)],
            buf_r.at[c, pl.ds(pl.multiple_of(mine * BLK, 16), BLK)],
            ssem.at[c, other],
            rsem.at[c, mine],
            {"expert": other},
        )

    def a2a_start(buf_s, buf_r, ssem, rsem, c):
        loop(NE, lambda d: a2a(buf_s, buf_r, ssem, rsem, c, (me + d) % NE, me).start(), 1)
        own = pl.ds(pl.multiple_of(me * BLK, 16), BLK)
        buf_r[c, own, :] = buf_s[c, own, :]

    def a2a_arrived(buf_s, buf_r, ssem, rsem, c):
        def arrived(d):
            src = (me + d) % NE
            a2a(buf_s, buf_r, ssem, rsem, c, src, src).wait_recv()

        loop(NE, arrived, 1)

    def a2a_sent(buf_s, buf_r, ssem, rsem, c):
        loop(NE, lambda d: a2a(buf_s, buf_r, ssem, rsem, c, (me + d) % NE, me).wait_send(), 1)

    def pack(buf, c):
        def part(i):
            r = pl.ds(pl.multiple_of(i * BLK, 16), BLK)
            buf[c, r, :] = stage[r, :].astype(BF16)

        loop(SLAB, part)

    def unpack(buf, c):
        def part(i):
            r = pl.ds(pl.multiple_of(i * BLK, 16), BLK)
            stage[r, :] = buf[c, r, :].astype(F32)

        loop(SLAB, part)

    for c in range(4):
        if c == 0:
            loads[0].wait()
        if c == 2:
            loads[1].wait()
        for k in range(SLAB):
            cols = pl.ds((c % 2) * CH + k * LANES, LANES)
            if c < 2:
                rows = tok[:, cols]
            else:
                rows = (gw_ref[...] * cot[:, cols].astype(F32)).astype(BF16)
            stage[pl.ds(k, BLK, stride=SLAB), :] = nn_dot(perm[pl.ds(0, BLK), :], rows)
        pack(send, c)
        a2a_start(send, recv, a_ssem, a_rsem, c)

    def gather(c, kind):
        buf = (xa, ga)[c // 2]
        cols = pl.ds((c % 2) * CH, CH)
        frm, to, peer = ((0, 2, x_peer), (0, 1, y_peer), (2, 3, y_peer))[kind]
        return remote(
            buf.at[pl.ds(frm * BLK, BLK), cols],
            buf.at[pl.ds(to * BLK, BLK), cols],
            g_ssem.at[c, kind],
            g_rsem.at[c, kind],
            peer,
        )

    def forward(c):
        gather(c, 0).wait_recv()
        gather(c, 2).start()

    for c in range(4):
        a2a_arrived(send, recv, a_ssem, a_rsem, c)
        unpack(recv, c)
        buf = (xa, ga)[c // 2]
        for k in range(SLAB):
            cols = pl.ds((c % 2) * CH + k * LANES, LANES)
            buf[pl.ds(0, BLK), cols] = stage[pl.ds(k, BLK, stride=SLAB), :].astype(BF16)
        gather(c, 0).start()
        gather(c, 1).start()
        if c > 0:
            forward(c - 1)
    forward(3)

    for c in loads[2:]:
        c.wait()
    for c in w_copies[:2]:
        c.wait_recv()

    pre[...] = jnp.zeros_like(pre)
    hg[...] = jnp.zeros_like(hg)
    for c in range(4):
        gather(c, 1).wait_recv()
        gather(c, 2).wait_recv()
        if c == 2:
            w_copies[2].wait_recv()
        buf, w, acc = ((xa, wgu, pre), (ga, wd, hg))[c // 2]

        def part(k, c=c, buf=buf, w=w, acc=acc):
            cols = pl.ds(pl.multiple_of((c % 2) * CH + k * TC, TC), TC)
            acc[...] += nt_dot(buf[:, cols], w[:, cols])

        loop(PER, part)

    def slopes(i):
        r = pl.ds(pl.multiple_of(i * 48, 16), 48)
        a = pre[r, 0 : 2 * FB]
        u = pre[r, 2 * FB : 4 * FB]
        h = hg[r, :]
        sig = jax.nn.sigmoid(a)
        act = a * sig
        hid[r, :] = (act * u).astype(BF16)
        gu[r, 0 : 2 * FB] = (h * u * (sig * (1.0 + a * (1.0 - sig)))).astype(BF16)
        gu[r, 2 * FB : 4 * FB] = (h * act).astype(BF16)

    loop(ROWS // 48, slopes)

    gut = gu[...].T
    hidt = hid[...].T
    dt[0:FB, :] = gut[FB : 2 * FB]
    dt[FB : 2 * FB, :] = gut[3 * FB : 4 * FB]
    dt[2 * FB : 3 * FB, :] = hidt[FB : 2 * FB]
    dt[3 * FB : 4 * FB, :] = gut[0:FB]
    dt[4 * FB : 5 * FB, :] = gut[2 * FB : 3 * FB]
    dt[5 * FB : 6 * FB, :] = hidt[0:FB]

    def tail_cols(j):
        return pl.ds(pl.multiple_of(j * TC, TC), TC)

    def x_sum(j):
        cols = tail_cols(j)
        return remote(tx.at[:, cols], rtx.at[:, cols], x_ssem.at[j], x_rsem.at[j], x_peer)

    def y_sum(j):
        cols = tail_cols(j)
        return remote(ty.at[:, cols], rty.at[:, cols], y_ssem.at[j], y_rsem.at[j], y_peer)

    def d_sum(j):
        cols = tail_cols(j)
        return remote(dsend.at[:, cols], drecv.at[:, cols], d_ssem.at[j], d_rsem.at[j], w_peer)

    def weights_out(j):
        cols = tail_cols(j)
        return [
            pltpu.make_async_copy(drecv.at[pl.ds(m * FB, FB), cols], o.at[0, :, cols], out_sem.at[m, j])
            for m, o in enumerate((og_hbm, ou_hbm, od_hbm))
        ]

    def other_weights(j):
        cols = tail_cols(j)
        dsend[0 : 2 * FB, cols] = nn_dot(dt[0 : 2 * FB, :], xa[:, cols]).astype(BF16)
        dsend[2 * FB : 3 * FB, cols] = nn_dot(dt[2 * FB : 3 * FB, :], ga[:, cols]).astype(BF16)
        d_sum(j).start()

    def own_weights(j):
        cols = tail_cols(j)
        d_sum(j).wait_recv()
        a = nn_dot(dt[3 * FB : 5 * FB, :], xa[:, cols])
        drecv[0 : 2 * FB, cols] = (a + drecv[0 : 2 * FB, cols].astype(F32)).astype(BF16)
        b = nn_dot(dt[5 * FB : 6 * FB, :], ga[:, cols])
        drecv[2 * FB : 3 * FB, cols] = (b + drecv[2 * FB : 3 * FB, cols].astype(F32)).astype(BF16)
        for c in weights_out(j):
            c.start()

    def x_part(j):
        cols = tail_cols(j)
        tx[:, cols] = nn_dot(gu[2 * BLK : 4 * BLK, :], wgu[:, cols]).astype(BF16)
        x_sum(j).start()

    def y_part(j):
        cols = tail_cols(j)
        x_sum(j).wait_recv()
        t = nn_dot(gu[BLK : 2 * BLK, :], wgu[:, cols])
        ty[:, cols] = (t + rtx[BLK : 2 * BLK, cols].astype(F32)).astype(BF16)
        y_sum(j).start()

    for c in range(4):
        a2a_sent(send, recv, a_ssem, a_rsem, c)

    def own_part(j):
        cols = tail_cols(j)
        y_sum(j).wait_recv()
        t = nn_dot(gu[0:BLK, :], wgu[:, cols])
        t = t + rtx[0:BLK, cols].astype(F32) + rty[:, cols].astype(F32)
        for i in range(TC // LANES):
            stage[pl.ds((j % PER) * (TC // LANES) + i, BLK, stride=SLAB), :] = t[:, i * LANES : (i + 1) * LANES]

        for b in range(2):

            @pl.when(j == b * PER + PER - 1)
            def _():
                pack(send, b)
                a2a_start(send, back, b_ssem, b_rsem, b)

    EARLY = 2
    LAG = 2

    def first(j):
        x_part(j)

        @pl.when(j < EARLY)
        def _():
            other_weights(j)

    loop(NT, first)

    def second(j):
        @pl.when(j < NT)
        def _():
            y_part(j)

        @pl.when(j + EARLY < NT)
        def _():
            other_weights(j + EARLY)

        @pl.when((j >= 1) & (j < NT + 1))
        def _():
            own_part(j - 1)

        @pl.when(j >= LAG)
        def _():
            own_weights(j - LAG)

    loop(NT + LAG, second)

    tg_out = [
        pltpu.make_async_copy(tg.at[:, pl.ds(b * CH, CH)], tg_hbm.at[:, pl.ds(b * CH, CH)], tok_sem.at[b])
        for b in range(2)
    ]
    for b in range(2):
        a2a_arrived(send, back, b_ssem, b_rsem, b)
        unpack(back, b)
        for k in range(SLAB):
            rows = stage[pl.ds(k, BLK, stride=SLAB), :].astype(BF16)
            tg[:, pl.ds(b * CH + k * LANES, LANES)] = nn_dot(pt[:, 0:BLK], rows).astype(BF16)
        tg_out[b].start()

    for c in w_copies:
        c.wait_send()
    for c in range(4):
        for kind in range(3):
            gather(c, kind).wait_send()
    for b in range(2):
        a2a_sent(send, back, b_ssem, b_rsem, b)

    def drain(j):
        x_sum(j).wait_send()
        y_sum(j).wait_send()
        d_sum(j).wait_send()
        for c in weights_out(j):
            c.wait()

    loop(NT, drain)
    for c in tg_out:
        c.wait()


def local(tokens, cotangent, expert_ids, gate_weights, gate_proj, up_proj, down_proj):
    hbm = pl.BlockSpec(memory_space=pl.ANY)
    vmem = pl.BlockSpec(memory_space=pltpu.VMEM)
    dma = pltpu.SemaphoreType.DMA
    wide = jax.ShapeDtypeStruct((1, FB, D), BF16)
    return pl.pallas_call(
        kernel,
        out_shape=(jax.ShapeDtypeStruct((TOK, D), BF16), wide, wide, wide),
        in_specs=[hbm, hbm, vmem, vmem, hbm, hbm, hbm],
        out_specs=(hbm, hbm, hbm, hbm),
        scratch_shapes=[
            pltpu.VMEM((TOK, D), BF16),
            pltpu.VMEM((TOK, D), BF16),
            pltpu.VMEM((TOK, 2 * LANES), BF16),
            pltpu.VMEM((2 * LANES, TOK), BF16),
            pltpu.VMEM((4 * FB, D), BF16),
            pltpu.VMEM((2 * FB, D), BF16),
            pltpu.VMEM((4, PACK, LANES), BF16),
            pltpu.VMEM((4, PACK, LANES), BF16),
            pltpu.VMEM((PACK, LANES), F32),
            pltpu.VMEM((ROWS, D), BF16),
            pltpu.VMEM((ROWS, D), BF16),
            pltpu.VMEM((ROWS, 4 * FB), F32),
            pltpu.VMEM((ROWS, 2 * FB), F32),
            pltpu.VMEM((ROWS, 4 * FB), BF16),
            pltpu.VMEM((ROWS, 2 * FB), BF16),
            pltpu.VMEM((6 * FB, ROWS), BF16),
            pltpu.VMEM((2 * BLK, D), BF16),
            pltpu.VMEM((2 * BLK, D), BF16),
            pltpu.VMEM((BLK, D), BF16),
            pltpu.VMEM((BLK, D), BF16),
            pltpu.VMEM((3 * FB, D), BF16),
            pltpu.VMEM((3 * FB, D), BF16),
            pltpu.VMEM((2, PACK, LANES), BF16),
            pltpu.VMEM((TOK, D), BF16),
            dma((5,)),
            dma((3,)),
            dma((3,)),
            dma((4, NE)),
            dma((4, NE)),
            dma((4, 3)),
            dma((4, 3)),
            dma((NT,)),
            dma((NT,)),
            dma((NT,)),
            dma((NT,)),
            dma((NT,)),
            dma((NT,)),
            dma((2, NE)),
            dma((2, NE)),
            dma((3, NT)),
            dma((2,)),
        ],
        cost_estimate=pl.CostEstimate(flops=14_500_000_000, bytes_accessed=12_500_000, transcendentals=300_000),
        compiler_params=pltpu.CompilerParams(
            collective_id=0, has_side_effects=True, vmem_limit_bytes=60 * 2**20
        ),
    )(tokens, cotangent, expert_ids, gate_weights, gate_proj, up_proj, down_proj)


def solution(mesh):
    rows = P(("group", "resp", "expert"), None)
    weights = P("expert", "resp", None)
    grads = P(("group", "expert"), "resp", None)
    return jax.shard_map(
        local,
        mesh=mesh,
        in_specs=(rows, rows, rows, rows, weights, weights, weights),
        out_specs=(rows, grads, grads, grads),
        check_vma=False,
    )
```

```python
import jax
import jax.numpy as jnp
from jax import lax
from jax.experimental import pallas as pl
from jax.experimental.pallas import tpu as pltpu
from jax.sharding import PartitionSpec as P

MESH = pl.DeviceIdType.MESH
BF16 = jnp.bfloat16
F32 = jnp.float32

TOK = 128
D = 4096
NE = 16
NZ = 8
CAP = 9
BLK = NE * CAP
HALF = NZ * CAP
FB = 192
ROWS = 4 * BLK
CH = 2048
LANES = 128
SLAB = CH // LANES
ZBLK = 2 * CAP * SLAB
EBLK = CAP * SLAB
GC = 1024
NG = D // GC
BSLAB = GC // LANES
BBLK = 2 * CAP * BSLAB
TC = 512
NT = D // TC
Y_FIRST = (1, 2)
EARLY = 8
LAG = 3


def nt_dot(a, b):
    return lax.dot_general(a, b, (((1,), (1,)), ((), ())), preferred_element_type=F32)


def nn_dot(a, b):
    return jnp.dot(a, b, preferred_element_type=F32)


def loop(n, body, first=0):
    def step(i, carry):
        body(i)
        return carry

    lax.fori_loop(first, n, step, 0)


def kernel(
    tok_hbm, cot_hbm, ids_ref, gw_ref, wg_hbm, wu_hbm, wd_hbm,
    tg_hbm, og_hbm, ou_hbm, od_hbm,
    tok, cot, pt, perm, order, wgu, wd, send, recv, over_y, over_x, over_yx, stage, xa, ga,
    pre, hg, gu, hid, dt, tx, rtx, kept, ty, rty, dsend, drecv, back,
    load_sem, w_ssem, w_rsem, a_ssem, a_rsem, p_ssem, p_rsem, q_ssem, q_rsem, g_ssem, g_rsem, h_ssem, h_rsem,
    x_ssem, x_rsem, y_ssem, y_rsem, d_ssem, d_rsem, e_ssem, e_rsem, b_ssem, b_rsem,
    out_sem, tok_sem,
):
    resp = lax.axis_index("resp")
    expert = lax.axis_index("expert")
    core = lax.axis_index("group")
    y = resp // 2
    z = expert // 2
    x_lo = expert % 2
    x = (resp % 2) * 2 + x_lo
    side = (y + core) % 2

    def at(y, x, z):
        return {"resp": y * 2 + x // 2, "expert": z * 2 + x % 2}

    y_peer = at((y + 1 + 2 * side) % 4, x, z)
    w_peer = at((y + 3 + 2 * side) % 4, x, z)
    x_peers = [at(y, (x + d) % 4, z) for d in (2, 1, 3)]
    lands = (0, 2, 1)

    def remote(src, dst, ssem, rsem, to):
        return pltpu.make_async_remote_copy(
            src_ref=src, dst_ref=dst, send_sem=ssem, recv_sem=rsem, device_id=to, device_id_type=MESH
        )

    loads = [
        pltpu.make_async_copy(tok_hbm, tok, load_sem.at[0]),
        pltpu.make_async_copy(cot_hbm, cot, load_sem.at[1]),
        pltpu.make_async_copy(wg_hbm.at[0], wgu.at[pl.ds(0, FB)], load_sem.at[2]),
        pltpu.make_async_copy(wu_hbm.at[0], wgu.at[pl.ds(2 * FB, FB)], load_sem.at[3]),
        pltpu.make_async_copy(wd_hbm.at[0], wd.at[pl.ds(0, FB)], load_sem.at[4]),
    ]
    for c in loads:
        c.start()

    barrier = pltpu.get_barrier_semaphore()
    for peer in [y_peer, w_peer] + x_peers:
        pl.semaphore_signal(barrier, inc=1, device_id=peer, device_id_type=MESH)

    def greet(d):
        pl.semaphore_signal(barrier, inc=1, device_id=at(y, x, (z + d) % NZ), device_id_type=MESH)

    loop(NZ, greet, 1)

    ids = ids_ref[...]
    ids = ids + x_lo * (1 - 2 * (ids & 1))
    lane = lax.broadcasted_iota(jnp.int32, (TOK, TOK), 1)
    row = lax.broadcasted_iota(jnp.int32, (TOK, TOK), 0)
    onehot = jnp.where(row == ids, 1.0, 0.0).astype(F32)
    upper = jnp.where(row < lane, 1.0, 0.0).astype(BF16)
    rank = jnp.sum(nn_dot(onehot.astype(BF16), upper) * onehot, axis=0, keepdims=True).astype(jnp.int32)
    slot = lax.broadcasted_iota(jnp.int32, (2 * LANES, TOK), 0)
    chosen = jnp.where(slot == ids * CAP + rank, 1.0, 0.0).astype(F32)
    perm[...] = chosen.astype(BF16)
    pt[...] = chosen.T.astype(BF16)
    scale = jnp.sum(chosen * gw_ref[...], axis=1, keepdims=True)[0:BLK]
    to = lax.broadcasted_iota(jnp.int32, (BLK, 2 * LANES), 0)
    frm = lax.broadcasted_iota(jnp.int32, (BLK, 2 * LANES), 1)
    to_z = (to * 57) >> 10
    rest = to - to_z * (2 * CAP)
    rest = jnp.where(rest >= CAP, rest - CAP + HALF, rest)
    order[...] = jnp.where(frm == rest + to_z * CAP, 1.0, 0.0).astype(BF16)

    def there(c, other, mine):
        return remote(
            send.at[c, other], recv.at[c, mine], a_ssem.at[c, other], a_rsem.at[c, mine], at(y, x, other)
        )

    def home(c, other, mine):
        return remote(
            send.at[c, other, pl.ds(0, BBLK)], back.at[c, mine], b_ssem.at[c, other], b_rsem.at[c, mine],
            at(y, x, other),
        )

    def a2a_start(way, c):
        loop(NZ, lambda d: way(c, (z + d) % NZ, z).start(), 1)

    def a2a_arrived(way, c):
        def arrived(d):
            src = (z + d) % NZ
            way(c, src, src).wait_recv()

        loop(NZ, arrived, 1)

    def a2a_sent(way, c):
        loop(NZ, lambda d: way(c, (z + d) % NZ, z).wait_send(), 1)

    def pack(c, rows):
        def part(i):
            send[c, i, pl.ds(0, rows), :] = stage[pl.ds(pl.multiple_of(i * rows, 16), rows), :].astype(BF16)

        loop(NZ, part)

    def dispatch(c):
        for k in range(SLAB):
            cols = pl.ds((c % 2) * CH + k * LANES, LANES)
            if c < 2:
                rows = nn_dot(perm[pl.ds(0, BLK), :], tok[:, cols])
            else:
                rows = nn_dot(perm[pl.ds(0, BLK), :], cot[:, cols]) * scale
            stage[pl.ds(k, BLK, stride=SLAB), :] = rows
        pack(c, ZBLK)

    def dispatched(c):
        a2a_start(there, c)
        recv[c, z] = send[c, z]

    loads[0].wait()
    dispatch(0)
    pl.semaphore_wait(barrier, NZ + 4)

    w_copies = [
        remote(wg_hbm.at[0], wgu.at[pl.ds(FB, FB)], w_ssem.at[0], w_rsem.at[0], w_peer),
        remote(wu_hbm.at[0], wgu.at[pl.ds(3 * FB, FB)], w_ssem.at[1], w_rsem.at[1], w_peer),
        remote(wd_hbm.at[0], wd.at[pl.ds(FB, FB)], w_ssem.at[2], w_rsem.at[2], w_peer),
    ]
    dispatched(0)
    for c in w_copies:
        c.start()
    for c in range(1, 4):
        if c == 2:
            loads[1].wait()
        dispatch(c)
        dispatched(c)

    def halves(ref, i):
        return ref.at[:, pl.ds(i * EBLK, EBLK)]

    def by_x(c, s):
        return remote(
            halves(recv.at[c], min(s, 1)), over_x.at[c, lands[s]], p_ssem.at[c, s], p_rsem.at[c, lands[s]],
            x_peers[s],
        )

    def by_yx(c, s):
        f = Y_FIRST.index(c)
        return remote(
            halves(over_y.at[f], min(s, 1)), over_yx.at[f, lands[s]], q_ssem.at[f, s], q_rsem.at[f, lands[s]],
            x_peers[s],
        )

    def by_y(c):
        f = Y_FIRST.index(c)
        return remote(recv.at[c], over_y.at[f], h_ssem.at[f], h_rsem.at[f], y_peer)

    def by_xy(p):
        buf = (xa, ga)[p // NG]
        cols = pl.ds((p % NG) * GC, GC)
        return remote(
            buf.at[pl.ds(0, 2 * BLK), cols], buf.at[pl.ds(2 * BLK, 2 * BLK), cols],
            g_ssem.at[p], g_rsem.at[p], y_peer,
        )

    def unpack(c, first, own, others):
        buf = (xa, ga)[c // 2]

        def part(i):
            for s in range(4):
                r = pl.ds(pl.multiple_of((s * NZ + i) * EBLK, 16), EBLK)
                if s == 0:
                    stage[r, :] = own[i, pl.ds(0, EBLK), :].astype(F32)
                else:
                    stage[r, :] = others[s - 1, i].astype(F32)

        loop(NZ, part)
        for k in range(SLAB):
            cols = pl.ds((c % 2) * CH + k * LANES, LANES)
            buf[pl.ds(first, 2 * BLK), cols] = stage[pl.ds(k, 2 * BLK, stride=SLAB), :].astype(BF16)

    def onward(c):
        if c in Y_FIRST:
            by_y(c).wait_recv()
            for s in range(3):
                by_yx(c, s).start()
        else:
            for s in range(3):
                by_x(c, s).wait_recv()
            unpack(c, 0, recv.at[c], over_x.at[c])
            for p in (2 * c, 2 * c + 1):
                by_xy(p).start()

    def settle(c):
        if c in Y_FIRST:
            f = Y_FIRST.index(c)
            for s in range(3):
                by_x(c, s).wait_recv()
            unpack(c, 0, recv.at[c], over_x.at[c])
            for s in range(3):
                by_yx(c, s).wait_recv()
            unpack(c, 2 * BLK, over_y.at[f], over_yx.at[f])
        else:
            for p in (2 * c, 2 * c + 1):
                by_xy(p).wait_recv()

    for c in range(4):
        a2a_arrived(there, c)
        if c in Y_FIRST:
            by_y(c).start()
        for s in range(3):
            by_x(c, s).start()
        if c > 0:
            onward(c - 1)
    onward(3)

    for c in loads[2:]:
        c.wait()
    for c in w_copies[:2]:
        c.wait_recv()

    def piece(p, w, acc):
        if p % 2 == 0:
            settle(p // 2)
        buf = (xa, ga)[p // NG]

        def part(k):
            cols = pl.ds(pl.multiple_of((p % NG) * GC + k * TC, TC), TC)
            t = nt_dot(buf[:, cols], w[:, cols])
            acc[...] = t + acc[...]

        loop(GC // TC, part)

    pre[...] = jnp.zeros_like(pre)
    hg[...] = jnp.zeros_like(hg)
    for p in range(NG):
        piece(p, wgu, pre)

    def activate(i):
        r = pl.ds(pl.multiple_of(i * 48, 16), 48)
        a = pre[r, 0 : 2 * FB]
        u = pre[r, 2 * FB : 4 * FB]
        sig = jax.nn.sigmoid(a)
        act = a * sig
        hid[r, :] = (act * u).astype(BF16)
        pre[r, 0 : 2 * FB] = u * (sig * (1.0 + a * (1.0 - sig)))
        pre[r, 2 * FB : 4 * FB] = act

    loop(ROWS // 48, activate)
    hidt = hid[...].T
    dt[2 * FB : 3 * FB, :] = hidt[FB : 2 * FB]
    dt[5 * FB : 6 * FB, :] = hidt[0:FB]

    w_copies[2].wait_recv()

    def e_sum(b):
        cols = pl.ds(pl.multiple_of(b * GC, GC), GC)
        rows = pl.ds(2 * FB, FB)
        return remote(dsend.at[rows, cols], drecv.at[rows, cols], e_ssem.at[b], e_rsem.at[b], w_peer)

    for p in range(NG, 2 * NG):
        piece(p, wd, hg)
        if p < 2 * NG - 1:
            cols = pl.ds((p % NG) * GC, GC)
            dsend[2 * FB : 3 * FB, cols] = nn_dot(dt[2 * FB : 3 * FB, :], ga[:, cols]).astype(BF16)
    for b in range(NG - 1):
        e_sum(b).start()

    def slopes(i):
        r = pl.ds(pl.multiple_of(i * 48, 16), 48)
        h = hg[r, :]
        gu[r, 0 : 2 * FB] = (h * pre[r, 0 : 2 * FB]).astype(BF16)
        gu[r, 2 * FB : 4 * FB] = (h * pre[r, 2 * FB : 4 * FB]).astype(BF16)

    loop(ROWS // 48, slopes)

    def tail_cols(j):
        return pl.ds(pl.multiple_of(j * TC, TC), TC)

    def outgoing(s):
        return wd.at[pl.ds(s * BLK, BLK)] if s < 2 else tx

    def x_sum(j, s):
        cols = tail_cols(j)
        return remote(
            outgoing(s).at[:, cols], rtx.at[lands[s], :, cols], x_ssem.at[j, s], x_rsem.at[j, lands[s]], x_peers[s]
        )

    def y_sum(j):
        cols = tail_cols(j)
        return remote(ty.at[:, cols], rty.at[:, cols], y_ssem.at[j], y_rsem.at[j], y_peer)

    def d_sum(j):
        cols = tail_cols(j)
        rows = pl.ds(0, 2 * FB)
        return remote(dsend.at[rows, cols], drecv.at[rows, cols], d_ssem.at[j], d_rsem.at[j], w_peer)

    def weights_out(j):
        cols = tail_cols(j)
        return [
            pltpu.make_async_copy(drecv.at[pl.ds(m * FB, FB), cols], o.at[0, :, cols], out_sem.at[m, j])
            for m, o in enumerate((og_hbm, ou_hbm, od_hbm))
        ]

    def other_weights(j):
        cols = tail_cols(j)
        dsend[0 : 2 * FB, cols] = nn_dot(dt[0 : 2 * FB, :], xa[:, cols]).astype(BF16)
        d_sum(j).start()

    def own_weights(j):
        cols = tail_cols(j)
        d_sum(j).wait_recv()
        a = nn_dot(dt[3 * FB : 5 * FB, :], xa[:, cols])
        drecv[0 : 2 * FB, cols] = (a + drecv[0 : 2 * FB, cols].astype(F32)).astype(BF16)
        @pl.when(j % 2 == 0)
        def _():
            e_sum(j // 2).wait_recv()

        b = nn_dot(dt[5 * FB : 6 * FB, :], ga[:, cols])
        drecv[2 * FB : 3 * FB, cols] = (b + drecv[2 * FB : 3 * FB, cols].astype(F32)).astype(BF16)
        for c in weights_out(j):
            c.start()

    def x_part(j):
        cols = tail_cols(j)
        t = nn_dot(gu[...], wgu[:, cols])

        def of(s):
            return jnp.concatenate(
                [t[s * HALF : (s + 1) * HALF], t[2 * BLK + s * HALF : 2 * BLK + (s + 1) * HALF]], axis=0
            ).astype(BF16)

        for s in range(3):
            outgoing(s)[:, cols] = of(s + 1)
            x_sum(j, s).start()
        kept[:, cols] = of(0)

    def sums(j, first):
        cols = tail_cols(j)
        a = kept[:, cols].astype(F32) + rtx[0, :, cols].astype(F32)
        b = rtx[1, :, cols].astype(F32) + rtx[2, :, cols].astype(F32)
        return jnp.concatenate([a[first : first + HALF], b[first : first + HALF]], axis=0)

    def y_part(j):
        for s in range(3):
            x_sum(j, s).wait_recv()
        ty[:, tail_cols(j)] = sums(j, HALF).astype(BF16)
        y_sum(j).start()

    for c in range(4):
        a2a_sent(there, c)
        for s in range(3):
            by_x(c, s).wait_send()
        if c in Y_FIRST:
            by_y(c).wait_send()

    def own_part(j):
        y_sum(j).wait_recv()
        t = sums(j, 0) + rty[:, tail_cols(j)].astype(F32)
        t = nn_dot(order[:, 0:BLK], t.astype(BF16))
        for i in range(TC // LANES):
            stage[pl.ds((j % 2) * (TC // LANES) + i, BLK, stride=BSLAB), :] = t[:, i * LANES : (i + 1) * LANES]

        @pl.when(j % 2 == 1)
        def _():
            b = j // 2
            pack(b, BBLK)
            a2a_start(home, b)
            back[b, z] = send[b, z, pl.ds(0, BBLK), :]

    loop(NT, x_part)

    cols = pl.ds((NG - 1) * GC, GC)
    dsend[2 * FB : 3 * FB, cols] = nn_dot(dt[2 * FB : 3 * FB, :], ga[:, cols]).astype(BF16)
    e_sum(NG - 1).start()
    gut = gu[...].T
    dt[0:FB, :] = gut[FB : 2 * FB]
    dt[FB : 2 * FB, :] = gut[3 * FB : 4 * FB]
    dt[3 * FB : 4 * FB, :] = gut[0:FB]
    dt[4 * FB : 5 * FB, :] = gut[2 * FB : 3 * FB]
    loop(EARLY, other_weights)

    def second(j):
        @pl.when(j < NT)
        def _():
            y_part(j)

        @pl.when(j + EARLY < NT)
        def _():
            other_weights(j + EARLY)

        @pl.when((j >= 1) & (j < NT + 1))
        def _():
            own_part(j - 1)

        @pl.when(j >= LAG)
        def _():
            own_weights(j - LAG)

    loop(NT + LAG, second)

    def tokens_out(b):
        cols = pl.ds(b * GC, GC)
        return pltpu.make_async_copy(tok.at[:, cols], tg_hbm.at[:, cols], tok_sem.at[b])

    for b in range(NG):
        a2a_arrived(home, b)

        def part(i, b=b):
            stage[pl.ds(pl.multiple_of(i * BBLK, 16), BBLK), :] = back[b, i].astype(F32)

        loop(NZ, part)
        for k in range(BSLAB):
            rows = stage[pl.ds(k, BLK, stride=BSLAB), :].astype(BF16)
            tok[:, pl.ds(b * GC + k * LANES, LANES)] = nn_dot(pt[:, 0:BLK], rows).astype(BF16)
        tokens_out(b).start()

    for c in w_copies:
        c.wait_send()
    for c in range(4):
        if c in Y_FIRST:
            for s in range(3):
                by_yx(c, s).wait_send()
        else:
            for p in (2 * c, 2 * c + 1):
                by_xy(p).wait_send()
    for b in range(NG):
        a2a_sent(home, b)
        e_sum(b).wait_send()

    def drain(j):
        for s in range(3):
            x_sum(j, s).wait_send()
        y_sum(j).wait_send()
        d_sum(j).wait_send()
        for c in weights_out(j):
            c.wait()

    loop(NT, drain)
    for b in range(NG):
        tokens_out(b).wait()


def copy_out(*refs):
    src, dst, held = refs[0:4], refs[4:8], refs[8:12]
    in_sem, out_sem = refs[12:]

    def parts(a, i):
        n = held[a].shape[0] // 4
        r = pl.ds(i * n, n)
        at = (r,) if a == 0 else (0, r)
        return (
            pltpu.make_async_copy(src[a].at[at], held[a].at[r], in_sem.at[a, i]),
            pltpu.make_async_copy(held[a].at[r], dst[a].at[at], out_sem.at[a, i]),
        )

    every = [parts(a, i) for a in range(4) for i in range(4)]
    for c, _ in every:
        c.start()
    for c, d in every:
        c.wait()
        d.start()
    for _, d in every:
        d.wait()


def local(tokens, cotangent, expert_ids, gate_weights, gate_proj, up_proj, down_proj):
    hbm = pl.BlockSpec(memory_space=pl.ANY)
    vmem = pl.BlockSpec(memory_space=pltpu.VMEM)
    dma = pltpu.SemaphoreType.DMA
    wide = jax.ShapeDtypeStruct((1, FB, D), BF16)
    outs = (jax.ShapeDtypeStruct((TOK, D), BF16), wide, wide, wide)
    done = pl.pallas_call(
        kernel,
        out_shape=outs,
        in_specs=[hbm, hbm, vmem, vmem, hbm, hbm, hbm],
        out_specs=(hbm, hbm, hbm, hbm),
        scratch_shapes=[
            pltpu.VMEM((TOK, D), BF16),
            pltpu.VMEM((TOK, D), BF16),
            pltpu.VMEM((TOK, 2 * LANES), BF16),
            pltpu.VMEM((2 * LANES, TOK), BF16),
            pltpu.VMEM((BLK, 2 * LANES), BF16),
            pltpu.VMEM((4 * FB, D), BF16),
            pltpu.VMEM((2 * FB, D), BF16),
            pltpu.VMEM((4, NZ, ZBLK, LANES), BF16),
            pltpu.VMEM((4, NZ, ZBLK, LANES), BF16),
            pltpu.VMEM((len(Y_FIRST), NZ, ZBLK, LANES), BF16),
            pltpu.VMEM((4, 3, NZ, EBLK, LANES), BF16),
            pltpu.VMEM((len(Y_FIRST), 3, NZ, EBLK, LANES), BF16),
            pltpu.VMEM((4 * NZ * EBLK, LANES), F32),
            pltpu.VMEM((ROWS, D), BF16),
            pltpu.VMEM((ROWS, D), BF16),
            pltpu.VMEM((ROWS, 4 * FB), F32),
            pltpu.VMEM((ROWS, 2 * FB), F32),
            pltpu.VMEM((ROWS, 4 * FB), BF16),
            pltpu.VMEM((ROWS, 2 * FB), BF16),
            pltpu.VMEM((6 * FB, ROWS), BF16),
            pltpu.VMEM((BLK, D), BF16),
            pltpu.VMEM((3, BLK, D), BF16),
            pltpu.VMEM((BLK, D), BF16),
            pltpu.VMEM((BLK, D), BF16),
            pltpu.VMEM((BLK, D), BF16),
            pltpu.VMEM((3 * FB, D), BF16),
            pltpu.VMEM((3 * FB, D), BF16),
            pltpu.VMEM((NG, NZ, BBLK, LANES), BF16),
            dma((5,)),
            dma((3,)),
            dma((3,)),
            dma((4, NZ)),
            dma((4, NZ)),
            dma((4, 3)),
            dma((4, 3)),
            dma((len(Y_FIRST), 3)),
            dma((len(Y_FIRST), 3)),
            dma((2 * NG,)),
            dma((2 * NG,)),
            dma((len(Y_FIRST),)),
            dma((len(Y_FIRST),)),
            dma((NT, 3)),
            dma((NT, 3)),
            dma((NT,)),
            dma((NT,)),
            dma((NT,)),
            dma((NT,)),
            dma((NG,)),
            dma((NG,)),
            dma((NG, NZ)),
            dma((NG, NZ)),
            dma((3, NT)),
            dma((NG,)),
        ],
        cost_estimate=pl.CostEstimate(flops=14_500_000_000, bytes_accessed=12_500_000, transcendentals=300_000),
        compiler_params=pltpu.CompilerParams(
            collective_id=0, has_side_effects=True, vmem_limit_bytes=62 * 2**20
        ),
    )(
        tokens, cotangent, expert_ids.reshape(1, TOK), gate_weights.reshape(1, TOK),
        gate_proj, up_proj, down_proj,
    )
    return pl.pallas_call(
        copy_out,
        out_shape=outs,
        in_specs=[hbm] * 4,
        out_specs=(hbm,) * 4,
        scratch_shapes=[pltpu.VMEM((TOK, D), BF16)] + [pltpu.VMEM((FB, D), BF16)] * 3 + [dma((4, 4)), dma((4, 4))],
    )(*done)


def solution(mesh):
    rows = P(("group", "resp", "expert"), None)
    weights = P("expert", "resp", None)
    grads = P(("group", "expert"), "resp", None)
    return jax.shard_map(
        local,
        mesh=mesh,
        in_specs=(rows, rows, rows, rows, weights, weights, weights),
        out_specs=(rows, grads, grads, grads),
        check_vma=False,
    )
```

```python
import jax
import jax.numpy as jnp
from jax import lax
from jax.experimental import pallas as pl
from jax.experimental.pallas import tpu as pltpu
from jax.sharding import PartitionSpec as P

MESH = pl.DeviceIdType.MESH
BF16 = jnp.bfloat16
F32 = jnp.float32

TOK = 128
D = 4096
NE = 16
NZ = 8
CAP = 9
BLK = NE * CAP
HALF = NZ * CAP
FB = 192
ROWS = 4 * BLK
CH = 2048
LANES = 128
SLAB = CH // LANES
ZBLK = 2 * CAP * SLAB
EBLK = CAP * SLAB
GC = 1024
NG = D // GC
BSLAB = GC // LANES
BBLK = 2 * CAP * BSLAB
TC = 512
NT = D // TC
Y_FIRST = (1, 2)
EARLY_DOWN = 2
EARLY = 8
LAG = 3


def nt_dot(a, b):
    return lax.dot_general(a, b, (((1,), (1,)), ((), ())), preferred_element_type=F32)


def nn_dot(a, b):
    return jnp.dot(a, b, preferred_element_type=F32)


def loop(n, body, first=0):
    def step(i, carry):
        body(i)
        return carry

    lax.fori_loop(first, n, step, 0)


def kernel(
    tok_hbm, cot_hbm, ids_ref, gw_ref, wg_hbm, wu_hbm, wd_hbm,
    tg_hbm, og_hbm, ou_hbm, od_hbm,
    tok, cot, pt, perm, order, wgu, wd, send, recv, ahead, over_y, over_x, over_yx, stage, xa, ga,
    pre, hg, gu, hid, dt, tx, rtx, kept, ty, rty, dsend, drecv, back,
    load_sem, w_ssem, w_rsem, a_ssem, a_rsem, f_ssem, f_rsem, p_ssem, p_rsem, q_ssem, q_rsem, g_ssem, g_rsem, h_ssem, h_rsem,
    x_ssem, x_rsem, y_ssem, y_rsem, d_ssem, d_rsem, e_ssem, e_rsem, b_ssem, b_rsem,
    out_sem, tok_sem,
):
    resp = lax.axis_index("resp")
    expert = lax.axis_index("expert")
    core = lax.axis_index("group")
    y = resp // 2
    z = expert // 2
    x_lo = expert % 2
    x = (resp % 2) * 2 + x_lo
    side = (y + core) % 2

    def at(y, x, z):
        return {"resp": y * 2 + x // 2, "expert": z * 2 + x % 2}

    y_peer = at((y + 1 + 2 * side) % 4, x, z)
    w_peer = at((y + 3 + 2 * side) % 4, x, z)
    x_peers = [at(y, (x + d) % 4, z) for d in (2, 1, 3)]
    lands = (0, 2, 1)

    def remote(src, dst, ssem, rsem, to):
        return pltpu.make_async_remote_copy(
            src_ref=src, dst_ref=dst, send_sem=ssem, recv_sem=rsem, device_id=to, device_id_type=MESH
        )

    loads = [
        pltpu.make_async_copy(tok_hbm, tok, load_sem.at[0]),
        pltpu.make_async_copy(cot_hbm, cot, load_sem.at[1]),
        pltpu.make_async_copy(wg_hbm.at[0], wgu.at[pl.ds(0, FB)], load_sem.at[2]),
        pltpu.make_async_copy(wu_hbm.at[0], wgu.at[pl.ds(2 * FB, FB)], load_sem.at[3]),
        pltpu.make_async_copy(wd_hbm.at[0], wd.at[pl.ds(0, FB)], load_sem.at[4]),
    ]
    for c in loads:
        c.start()

    barrier = pltpu.get_barrier_semaphore()
    for peer in [y_peer, w_peer] + x_peers:
        pl.semaphore_signal(barrier, inc=1, device_id=peer, device_id_type=MESH)

    def greet(d):
        pl.semaphore_signal(barrier, inc=1, device_id=at(y, x, (z + d) % NZ), device_id_type=MESH)

    loop(NZ, greet, 1)

    ids = ids_ref[...]
    ids = ids + x_lo * (1 - 2 * (ids & 1))
    lane = lax.broadcasted_iota(jnp.int32, (TOK, TOK), 1)
    row = lax.broadcasted_iota(jnp.int32, (TOK, TOK), 0)
    onehot = jnp.where(row == ids, 1.0, 0.0).astype(F32)
    upper = jnp.where(row < lane, 1.0, 0.0).astype(BF16)
    rank = jnp.sum(nn_dot(onehot.astype(BF16), upper) * onehot, axis=0, keepdims=True).astype(jnp.int32)
    slot = lax.broadcasted_iota(jnp.int32, (2 * LANES, TOK), 0)
    chosen = jnp.where(slot == ids * CAP + rank, 1.0, 0.0).astype(F32)
    perm[...] = chosen.astype(BF16)
    pt[...] = chosen.T.astype(BF16)
    scale = jnp.sum(chosen * gw_ref[...], axis=1, keepdims=True)[0:BLK]
    to = lax.broadcasted_iota(jnp.int32, (BLK, 2 * LANES), 0)
    frm = lax.broadcasted_iota(jnp.int32, (BLK, 2 * LANES), 1)
    to_z = (to * 57) >> 10
    rest = to - to_z * (2 * CAP)
    rest = jnp.where(rest >= CAP, rest - CAP + HALF, rest)
    order[...] = jnp.where(frm == rest + to_z * CAP, 1.0, 0.0).astype(BF16)

    def there(c, other, mine):
        return remote(
            send.at[c, other], recv.at[c, mine], a_ssem.at[c, other], a_rsem.at[c, mine], at(y, x, other)
        )

    def home(c, other, mine):
        return remote(
            send.at[c, other, pl.ds(0, BBLK)], back.at[c, mine], b_ssem.at[c, other], b_rsem.at[c, mine],
            at(y, x, other),
        )

    def a2a_start(way, c):
        loop(NZ, lambda d: way(c, (z + d) % NZ, z).start(), 1)

    def a2a_arrived(way, c):
        def arrived(d):
            src = (z + d) % NZ
            way(c, src, src).wait_recv()

        loop(NZ, arrived, 1)

    def a2a_sent(way, c):
        loop(NZ, lambda d: way(c, (z + d) % NZ, z).wait_send(), 1)

    def halves(ref, i):
        return ref.at[:, pl.ds(i * EBLK, EBLK)]

    def ahead_x(s):
        return remote(
            halves(send.at[0], min(s, 1)), ahead.at[lands[s]], p_ssem.at[0, s], p_rsem.at[0, lands[s]], x_peers[s]
        )

    def ahead_z(s, other, mine):
        if s == 0:
            src, dst = send.at[0, other, pl.ds(0, EBLK)], recv.at[0, mine, pl.ds(0, EBLK)]
        else:
            src, dst = ahead.at[s - 1, other], over_x.at[0, s - 1, mine]
        return remote(src, dst, f_ssem.at[s, other], f_rsem.at[s, mine], at(y, x, other))

    def pack(c, rows):
        def part(i):
            send[c, i, pl.ds(0, rows), :] = stage[pl.ds(pl.multiple_of(i * rows, 16), rows), :].astype(BF16)

        loop(NZ, part)

    def dispatch(c):
        for k in range(SLAB):
            cols = pl.ds((c % 2) * CH + k * LANES, LANES)
            if c < 2:
                rows = nn_dot(perm[pl.ds(0, BLK), :], tok[:, cols])
            else:
                rows = nn_dot(perm[pl.ds(0, BLK), :], cot[:, cols]) * scale
            stage[pl.ds(k, BLK, stride=SLAB), :] = rows
        pack(c, ZBLK)

    def dispatched(c):
        a2a_start(there, c)
        recv[c, z] = send[c, z]

    loads[0].wait()
    dispatch(0)
    pl.semaphore_wait(barrier, NZ + 4)

    w_copies = [
        remote(wg_hbm.at[0], wgu.at[pl.ds(FB, FB)], w_ssem.at[0], w_rsem.at[0], w_peer),
        remote(wu_hbm.at[0], wgu.at[pl.ds(3 * FB, FB)], w_ssem.at[1], w_rsem.at[1], w_peer),
        remote(wd_hbm.at[0], wd.at[pl.ds(FB, FB)], w_ssem.at[2], w_rsem.at[2], w_peer),
    ]
    for s in range(3):
        ahead_x(s).start()
    a2a_start(ahead_z, 0)
    recv[0, z, pl.ds(0, EBLK), :] = send[0, z, pl.ds(0, EBLK), :]
    for c in w_copies:
        c.start()
    for c in range(1, 4):
        if c == 2:
            loads[1].wait()
        dispatch(c)
        dispatched(c)

    for s in range(3):
        ahead_x(s).wait_recv()
        a2a_start(ahead_z, lands[s] + 1)
        over_x[0, lands[s], z] = ahead[lands[s], z]

    def by_x(c, s):
        return remote(
            halves(recv.at[c], min(s, 1)), over_x.at[c, lands[s]], p_ssem.at[c, s], p_rsem.at[c, lands[s]],
            x_peers[s],
        )

    def by_yx(c, s):
        f = Y_FIRST.index(c)
        return remote(
            halves(over_y.at[f], min(s, 1)), over_yx.at[f, lands[s]], q_ssem.at[f, s], q_rsem.at[f, lands[s]],
            x_peers[s],
        )

    def by_y(c):
        f = Y_FIRST.index(c)
        return remote(recv.at[c], over_y.at[f], h_ssem.at[f], h_rsem.at[f], y_peer)

    def by_xy(p):
        buf = (xa, ga)[p // NG]
        cols = pl.ds((p % NG) * GC, GC)
        return remote(
            buf.at[pl.ds(0, 2 * BLK), cols], buf.at[pl.ds(2 * BLK, 2 * BLK), cols],
            g_ssem.at[p], g_rsem.at[p], y_peer,
        )

    def unpack(c, first, own, others):
        buf = (xa, ga)[c // 2]

        def part(i):
            for s in range(4):
                r = pl.ds(pl.multiple_of((s * NZ + i) * EBLK, 16), EBLK)
                if s == 0:
                    stage[r, :] = own[i, pl.ds(0, EBLK), :].astype(F32)
                else:
                    stage[r, :] = others[s - 1, i].astype(F32)

        loop(NZ, part)
        for k in range(SLAB):
            cols = pl.ds((c % 2) * CH + k * LANES, LANES)
            buf[pl.ds(first, 2 * BLK), cols] = stage[pl.ds(k, 2 * BLK, stride=SLAB), :].astype(BF16)

    def onward(c):
        if c in Y_FIRST:
            by_y(c).wait_recv()
            for s in range(3):
                by_yx(c, s).start()
        else:
            for s in range(4):
                if c == 0:
                    a2a_arrived(ahead_z, s)
                elif s < 3:
                    by_x(c, s).wait_recv()
            unpack(c, 0, recv.at[c], over_x.at[c])
            for p in (2 * c, 2 * c + 1):
                by_xy(p).start()

    def settle(c):
        if c in Y_FIRST:
            f = Y_FIRST.index(c)
            for s in range(3):
                by_x(c, s).wait_recv()
            unpack(c, 0, recv.at[c], over_x.at[c])
            for s in range(3):
                by_yx(c, s).wait_recv()
            unpack(c, 2 * BLK, over_y.at[f], over_yx.at[f])
        else:
            for p in (2 * c, 2 * c + 1):
                by_xy(p).wait_recv()

    for c in range(1, 4):
        a2a_arrived(there, c)
        if c in Y_FIRST:
            by_y(c).start()
        for s in range(3):
            by_x(c, s).start()
        if c > 1:
            onward(c - 1)
    onward(0)
    onward(3)

    for c in loads[2:]:
        c.wait()
    for c in w_copies[:2]:
        c.wait_recv()

    def piece(p, w, acc):
        if p % 2 == 0:
            settle(p // 2)
        buf = (xa, ga)[p // NG]

        def part(k):
            cols = pl.ds(pl.multiple_of((p % NG) * GC + k * TC, TC), TC)
            t = nt_dot(buf[:, cols], w[:, cols])
            acc[...] = t + acc[...]

        loop(GC // TC, part)

    pre[...] = jnp.zeros_like(pre)
    hg[...] = jnp.zeros_like(hg)
    for p in range(NG):
        piece(p, wgu, pre)

    def activate(i):
        r = pl.ds(pl.multiple_of(i * 48, 16), 48)
        a = pre[r, 0 : 2 * FB]
        u = pre[r, 2 * FB : 4 * FB]
        sig = jax.nn.sigmoid(a)
        act = a * sig
        hid[r, :] = (act * u).astype(BF16)
        pre[r, 0 : 2 * FB] = u * (sig * (1.0 + a * (1.0 - sig)))
        pre[r, 2 * FB : 4 * FB] = act

    loop(ROWS // 48, activate)
    hidt = hid[...].T
    dt[2 * FB : 3 * FB, :] = hidt[FB : 2 * FB]
    dt[5 * FB : 6 * FB, :] = hidt[0:FB]

    w_copies[2].wait_recv()

    def e_sum(b):
        cols = pl.ds(pl.multiple_of(b * GC, GC), GC)
        rows = pl.ds(2 * FB, FB)
        return remote(dsend.at[rows, cols], drecv.at[rows, cols], e_ssem.at[b], e_rsem.at[b], w_peer)

    for p in range(NG, 2 * NG):
        piece(p, wd, hg)
        if p < 2 * NG - 1:
            cols = pl.ds((p % NG) * GC, GC)
            dsend[2 * FB : 3 * FB, cols] = nn_dot(dt[2 * FB : 3 * FB, :], ga[:, cols]).astype(BF16)
            if p - NG < EARLY_DOWN:
                e_sum(p - NG).start()
    for b in range(EARLY_DOWN, NG - 1):
        e_sum(b).start()

    def slopes(i):
        r = pl.ds(pl.multiple_of(i * 48, 16), 48)
        h = hg[r, :]
        gu[r, 0 : 2 * FB] = (h * pre[r, 0 : 2 * FB]).astype(BF16)
        gu[r, 2 * FB : 4 * FB] = (h * pre[r, 2 * FB : 4 * FB]).astype(BF16)

    loop(ROWS // 48, slopes)

    def tail_cols(j):
        return pl.ds(pl.multiple_of(j * TC, TC), TC)

    def outgoing(s):
        return wd.at[pl.ds(s * BLK, BLK)] if s < 2 else tx

    def x_sum(j, s):
        cols = tail_cols(j)
        return remote(
            outgoing(s).at[:, cols], rtx.at[lands[s], :, cols], x_ssem.at[j, s], x_rsem.at[j, lands[s]], x_peers[s]
        )

    def y_sum(j):
        cols = tail_cols(j)
        return remote(ty.at[:, cols], rty.at[:, cols], y_ssem.at[j], y_rsem.at[j], y_peer)

    def d_sum(j):
        cols = tail_cols(j)
        rows = pl.ds(0, 2 * FB)
        return remote(dsend.at[rows, cols], drecv.at[rows, cols], d_ssem.at[j], d_rsem.at[j], w_peer)

    def weights_out(j):
        cols = tail_cols(j)
        return [
            pltpu.make_async_copy(drecv.at[pl.ds(m * FB, FB), cols], o.at[0, :, cols], out_sem.at[m, j])
            for m, o in enumerate((og_hbm, ou_hbm, od_hbm))
        ]

    def other_weights(j):
        cols = tail_cols(j)
        dsend[0 : 2 * FB, cols] = nn_dot(dt[0 : 2 * FB, :], xa[:, cols]).astype(BF16)
        d_sum(j).start()

    def own_weights(j):
        cols = tail_cols(j)
        d_sum(j).wait_recv()
        a = nn_dot(dt[3 * FB : 5 * FB, :], xa[:, cols])
        drecv[0 : 2 * FB, cols] = (a + drecv[0 : 2 * FB, cols].astype(F32)).astype(BF16)
        @pl.when(j % 2 == 0)
        def _():
            e_sum(j // 2).wait_recv()

        b = nn_dot(dt[5 * FB : 6 * FB, :], ga[:, cols])
        drecv[2 * FB : 3 * FB, cols] = (b + drecv[2 * FB : 3 * FB, cols].astype(F32)).astype(BF16)
        for c in weights_out(j):
            c.start()

    def x_part(j):
        cols = tail_cols(j)
        t = nn_dot(gu[...], wgu[:, cols])

        def of(s):
            return jnp.concatenate(
                [t[s * HALF : (s + 1) * HALF], t[2 * BLK + s * HALF : 2 * BLK + (s + 1) * HALF]], axis=0
            ).astype(BF16)

        for s in range(3):
            outgoing(s)[:, cols] = of(s + 1)
            x_sum(j, s).start()
        kept[:, cols] = of(0)

    def sums(j, first):
        cols = tail_cols(j)
        a = kept[:, cols].astype(F32) + rtx[0, :, cols].astype(F32)
        b = rtx[1, :, cols].astype(F32) + rtx[2, :, cols].astype(F32)
        return jnp.concatenate([a[first : first + HALF], b[first : first + HALF]], axis=0)

    def y_part(j):
        for s in range(3):
            x_sum(j, s).wait_recv()
        ty[:, tail_cols(j)] = sums(j, HALF).astype(BF16)
        y_sum(j).start()

    for s in range(4):
        a2a_sent(ahead_z, s)
    for s in range(3):
        ahead_x(s).wait_send()
    for c in range(1, 4):
        a2a_sent(there, c)
        for s in range(3):
            by_x(c, s).wait_send()
        if c in Y_FIRST:
            by_y(c).wait_send()

    def own_part(j):
        y_sum(j).wait_recv()
        t = sums(j, 0) + rty[:, tail_cols(j)].astype(F32)
        t = nn_dot(order[:, 0:BLK], t.astype(BF16))
        for i in range(TC // LANES):
            stage[pl.ds((j % 2) * (TC // LANES) + i, BLK, stride=BSLAB), :] = t[:, i * LANES : (i + 1) * LANES]

        @pl.when(j % 2 == 1)
        def _():
            b = j // 2
            pack(b, BBLK)
            a2a_start(home, b)
            back[b, z] = send[b, z, pl.ds(0, BBLK), :]

    loop(NT, x_part)

    cols = pl.ds((NG - 1) * GC, GC)
    dsend[2 * FB : 3 * FB, cols] = nn_dot(dt[2 * FB : 3 * FB, :], ga[:, cols]).astype(BF16)
    e_sum(NG - 1).start()
    gut = gu[...].T
    dt[0:FB, :] = gut[FB : 2 * FB]
    dt[FB : 2 * FB, :] = gut[3 * FB : 4 * FB]
    dt[3 * FB : 4 * FB, :] = gut[0:FB]
    dt[4 * FB : 5 * FB, :] = gut[2 * FB : 3 * FB]
    loop(EARLY, other_weights)

    def second(j):
        @pl.when(j < NT)
        def _():
            y_part(j)

        @pl.when(j + EARLY < NT)
        def _():
            other_weights(j + EARLY)

        @pl.when((j >= 1) & (j < NT + 1))
        def _():
            own_part(j - 1)

        @pl.when(j >= LAG)
        def _():
            own_weights(j - LAG)

    loop(NT + LAG, second)

    def tokens_out(b):
        cols = pl.ds(b * GC, GC)
        return pltpu.make_async_copy(tok.at[:, cols], tg_hbm.at[:, cols], tok_sem.at[b])

    for b in range(NG):
        a2a_arrived(home, b)

        def part(i, b=b):
            stage[pl.ds(pl.multiple_of(i * BBLK, 16), BBLK), :] = back[b, i].astype(F32)

        loop(NZ, part)
        for k in range(BSLAB):
            rows = stage[pl.ds(k, BLK, stride=BSLAB), :].astype(BF16)
            tok[:, pl.ds(b * GC + k * LANES, LANES)] = nn_dot(pt[:, 0:BLK], rows).astype(BF16)
        tokens_out(b).start()

    for c in w_copies:
        c.wait_send()
    for c in range(4):
        if c in Y_FIRST:
            for s in range(3):
                by_yx(c, s).wait_send()
        else:
            for p in (2 * c, 2 * c + 1):
                by_xy(p).wait_send()
    for b in range(NG):
        a2a_sent(home, b)
        e_sum(b).wait_send()

    def drain(j):
        for s in range(3):
            x_sum(j, s).wait_send()
        y_sum(j).wait_send()
        d_sum(j).wait_send()
        for c in weights_out(j):
            c.wait()

    loop(NT, drain)
    for b in range(NG):
        tokens_out(b).wait()


def copy_out(*refs):
    src, dst, held = refs[0:4], refs[4:8], refs[8:12]
    in_sem, out_sem = refs[12:]

    def parts(a, i):
        n = held[a].shape[0] // 4
        r = pl.ds(i * n, n)
        at = (r,) if a == 0 else (0, r)
        return (
            pltpu.make_async_copy(src[a].at[at], held[a].at[r], in_sem.at[a, i]),
            pltpu.make_async_copy(held[a].at[r], dst[a].at[at], out_sem.at[a, i]),
        )

    every = [parts(a, i) for a in range(4) for i in range(4)]
    for c, _ in every:
        c.start()
    for c, d in every:
        c.wait()
        d.start()
    for _, d in every:
        d.wait()


def local(tokens, cotangent, expert_ids, gate_weights, gate_proj, up_proj, down_proj):
    hbm = pl.BlockSpec(memory_space=pl.ANY)
    vmem = pl.BlockSpec(memory_space=pltpu.VMEM)
    dma = pltpu.SemaphoreType.DMA
    wide = jax.ShapeDtypeStruct((1, FB, D), BF16)
    outs = (jax.ShapeDtypeStruct((TOK, D), BF16), wide, wide, wide)
    done = pl.pallas_call(
        kernel,
        out_shape=outs,
        in_specs=[hbm, hbm, vmem, vmem, hbm, hbm, hbm],
        out_specs=(hbm, hbm, hbm, hbm),
        scratch_shapes=[
            pltpu.VMEM((TOK, D), BF16),
            pltpu.VMEM((TOK, D), BF16),
            pltpu.VMEM((TOK, 2 * LANES), BF16),
            pltpu.VMEM((2 * LANES, TOK), BF16),
            pltpu.VMEM((BLK, 2 * LANES), BF16),
            pltpu.VMEM((4 * FB, D), BF16),
            pltpu.VMEM((2 * FB, D), BF16),
            pltpu.VMEM((4, NZ, ZBLK, LANES), BF16),
            pltpu.VMEM((4, NZ, ZBLK, LANES), BF16),
            pltpu.VMEM((3, NZ, EBLK, LANES), BF16),
            pltpu.VMEM((len(Y_FIRST), NZ, ZBLK, LANES), BF16),
            pltpu.VMEM((4, 3, NZ, EBLK, LANES), BF16),
            pltpu.VMEM((len(Y_FIRST), 3, NZ, EBLK, LANES), BF16),
            pltpu.VMEM((4 * NZ * EBLK, LANES), F32),
            pltpu.VMEM((ROWS, D), BF16),
            pltpu.VMEM((ROWS, D), BF16),
            pltpu.VMEM((ROWS, 4 * FB), F32),
            pltpu.VMEM((ROWS, 2 * FB), F32),
            pltpu.VMEM((ROWS, 4 * FB), BF16),
            pltpu.VMEM((ROWS, 2 * FB), BF16),
            pltpu.VMEM((6 * FB, ROWS), BF16),
            pltpu.VMEM((BLK, D), BF16),
            pltpu.VMEM((3, BLK, D), BF16),
            pltpu.VMEM((BLK, D), BF16),
            pltpu.VMEM((BLK, D), BF16),
            pltpu.VMEM((BLK, D), BF16),
            pltpu.VMEM((3 * FB, D), BF16),
            pltpu.VMEM((3 * FB, D), BF16),
            pltpu.VMEM((NG, NZ, BBLK, LANES), BF16),
            dma((5,)),
            dma((3,)),
            dma((3,)),
            dma((4, NZ)),
            dma((4, NZ)),
            dma((4, NZ)),
            dma((4, NZ)),
            dma((4, 3)),
            dma((4, 3)),
            dma((len(Y_FIRST), 3)),
            dma((len(Y_FIRST), 3)),
            dma((2 * NG,)),
            dma((2 * NG,)),
            dma((len(Y_FIRST),)),
            dma((len(Y_FIRST),)),
            dma((NT, 3)),
            dma((NT, 3)),
            dma((NT,)),
            dma((NT,)),
            dma((NT,)),
            dma((NT,)),
            dma((NG,)),
            dma((NG,)),
            dma((NG, NZ)),
            dma((NG, NZ)),
            dma((3, NT)),
            dma((NG,)),
        ],
        cost_estimate=pl.CostEstimate(flops=14_500_000_000, bytes_accessed=12_500_000, transcendentals=300_000),
        compiler_params=pltpu.CompilerParams(
            collective_id=0, has_side_effects=True, vmem_limit_bytes=62 * 2**20
        ),
    )(
        tokens, cotangent, expert_ids.reshape(1, TOK), gate_weights.reshape(1, TOK),
        gate_proj, up_proj, down_proj,
    )
    return pl.pallas_call(
        copy_out,
        out_shape=outs,
        in_specs=[hbm] * 4,
        out_specs=(hbm,) * 4,
        scratch_shapes=[pltpu.VMEM((TOK, D), BF16)] + [pltpu.VMEM((FB, D), BF16)] * 3 + [dma((4, 4)), dma((4, 4))],
    )(*done)


def solution(mesh):
    rows = P(("group", "resp", "expert"), None)
    weights = P("expert", "resp", None)
    grads = P(("group", "expert"), "resp", None)
    return jax.shard_map(
        local,
        mesh=mesh,
        in_specs=(rows, rows, rows, rows, weights, weights, weights),
        out_specs=(rows, grads, grads, grads),
        check_vma=False,
    )
```

```python
import jax
import jax.numpy as jnp
from jax import lax
from jax.experimental import pallas as pl
from jax.experimental.pallas import tpu as pltpu
from jax.sharding import PartitionSpec as P

MESH = pl.DeviceIdType.MESH
BF16 = jnp.bfloat16
F32 = jnp.float32

TOK = 128
D = 4096
NE = 16
NZ = 8
CAP = 9
BLK = NE * CAP
HALF = NZ * CAP
FB = 192
ROWS = 4 * BLK
CH = 2048
LANES = 128
SLAB = CH // LANES
ZBLK = 2 * CAP * SLAB
EBLK = CAP * SLAB
GC = 1024
NG = D // GC
BSLAB = GC // LANES
BBLK = 2 * CAP * BSLAB
TC = 512
NT = D // TC
Y_FIRST = (1, 2)
EARLY_DOWN = 3
EARLY = 8
HEAD = 2
LAG = 3


def nt_dot(a, b):
    return lax.dot_general(a, b, (((1,), (1,)), ((), ())), preferred_element_type=F32)


def nn_dot(a, b):
    return jnp.dot(a, b, preferred_element_type=F32)


def loop(n, body, first=0):
    def step(i, carry):
        body(i)
        return carry

    lax.fori_loop(first, n, step, 0)


def kernel(
    tok_hbm, cot_hbm, ids_ref, gw_ref, wg_hbm, wu_hbm, wd_hbm,
    tg_hbm, og_hbm, ou_hbm, od_hbm,
    tok, cot, pt, perm, order, wgu, wd, send, recv, ahead, over_y, over_x, over_yx, stage, xa, ga,
    pre, hg, gu, hid, dt, tx, rtx, kept, ty, rty, dsend, drecv, back,
    load_sem, w_ssem, w_rsem, a_ssem, a_rsem, f_ssem, f_rsem, p_ssem, p_rsem, q_ssem, q_rsem, g_ssem, g_rsem, h_ssem, h_rsem,
    x_ssem, x_rsem, y_ssem, y_rsem, d_ssem, d_rsem, e_ssem, e_rsem, b_ssem, b_rsem,
    out_sem, tok_sem,
):
    resp = lax.axis_index("resp")
    expert = lax.axis_index("expert")
    core = lax.axis_index("group")
    y = resp // 2
    z = expert // 2
    x_lo = expert % 2
    x = (resp % 2) * 2 + x_lo
    side = (y + core) % 2

    def at(y, x, z):
        return {"resp": y * 2 + x // 2, "expert": z * 2 + x % 2}

    y_peer = at((y + 1 + 2 * side) % 4, x, z)
    w_peer = at((y + 3 + 2 * side) % 4, x, z)
    x_peers = [at(y, (x + d) % 4, z) for d in (2, 1, 3)]
    lands = (0, 2, 1)

    def remote(src, dst, ssem, rsem, to):
        return pltpu.make_async_remote_copy(
            src_ref=src, dst_ref=dst, send_sem=ssem, recv_sem=rsem, device_id=to, device_id_type=MESH
        )

    loads = [
        pltpu.make_async_copy(tok_hbm, tok, load_sem.at[0]),
        pltpu.make_async_copy(cot_hbm, cot, load_sem.at[1]),
        pltpu.make_async_copy(wg_hbm.at[0], wgu.at[pl.ds(0, FB)], load_sem.at[2]),
        pltpu.make_async_copy(wu_hbm.at[0], wgu.at[pl.ds(2 * FB, FB)], load_sem.at[3]),
        pltpu.make_async_copy(wd_hbm.at[0], wd.at[pl.ds(0, FB)], load_sem.at[4]),
    ]
    for c in loads:
        c.start()

    barrier = pltpu.get_barrier_semaphore()
    for peer in [y_peer, w_peer] + x_peers:
        pl.semaphore_signal(barrier, inc=1, device_id=peer, device_id_type=MESH)

    def greet(d):
        pl.semaphore_signal(barrier, inc=1, device_id=at(y, x, (z + d) % NZ), device_id_type=MESH)

    loop(NZ, greet, 1)

    ids = ids_ref[...]
    ids = ids + x_lo * (1 - 2 * (ids & 1))
    lane = lax.broadcasted_iota(jnp.int32, (TOK, TOK), 1)
    row = lax.broadcasted_iota(jnp.int32, (TOK, TOK), 0)
    onehot = jnp.where(row == ids, 1.0, 0.0).astype(F32)
    upper = jnp.where(row < lane, 1.0, 0.0).astype(BF16)
    rank = jnp.sum(nn_dot(onehot.astype(BF16), upper) * onehot, axis=0, keepdims=True).astype(jnp.int32)
    slot = lax.broadcasted_iota(jnp.int32, (2 * LANES, TOK), 0)
    chosen = jnp.where(slot == ids * CAP + rank, 1.0, 0.0).astype(F32)
    perm[...] = chosen.astype(BF16)
    pt[...] = chosen.T.astype(BF16)
    scale = jnp.sum(chosen * gw_ref[...], axis=1, keepdims=True)[0:BLK]
    to = lax.broadcasted_iota(jnp.int32, (BLK, 2 * LANES), 0)
    frm = lax.broadcasted_iota(jnp.int32, (BLK, 2 * LANES), 1)
    to_z = (to * 57) >> 10
    rest = to - to_z * (2 * CAP)
    rest = jnp.where(rest >= CAP, rest - CAP + HALF, rest)
    order[...] = jnp.where(frm == rest + to_z * CAP, 1.0, 0.0).astype(BF16)

    def there(c, other, mine):
        return remote(
            send.at[c, other], recv.at[c, mine], a_ssem.at[c, other], a_rsem.at[c, mine], at(y, x, other)
        )

    def home(c, other, mine):
        return remote(
            send.at[c, other, pl.ds(0, BBLK)], back.at[c, mine], b_ssem.at[c, other], b_rsem.at[c, mine],
            at(y, x, other),
        )

    def a2a_start(way, c):
        loop(NZ, lambda d: way(c, (z + d) % NZ, z).start(), 1)

    def a2a_arrived(way, c):
        def arrived(d):
            src = (z + d) % NZ
            way(c, src, src).wait_recv()

        loop(NZ, arrived, 1)

    def a2a_sent(way, c):
        loop(NZ, lambda d: way(c, (z + d) % NZ, z).wait_send(), 1)

    def halves(ref, i):
        return ref.at[:, pl.ds(i * EBLK, EBLK)]

    def ahead_x(s):
        return remote(
            halves(send.at[0], min(s, 1)), ahead.at[lands[s]], p_ssem.at[0, s], p_rsem.at[0, lands[s]], x_peers[s]
        )

    def ahead_z(s, other, mine):
        if s == 0:
            src, dst = send.at[0, other, pl.ds(0, EBLK)], recv.at[0, mine, pl.ds(0, EBLK)]
        else:
            src, dst = ahead.at[s - 1, other], over_x.at[0, s - 1, mine]
        return remote(src, dst, f_ssem.at[s, other], f_rsem.at[s, mine], at(y, x, other))

    def pack(c, rows):
        def part(i):
            send[c, i, pl.ds(0, rows), :] = stage[pl.ds(pl.multiple_of(i * rows, 16), rows), :].astype(BF16)

        loop(NZ, part)

    def dispatch(c):
        for k in range(SLAB):
            cols = pl.ds((c % 2) * CH + k * LANES, LANES)
            if c < 2:
                rows = nn_dot(perm[pl.ds(0, BLK), :], tok[:, cols])
            else:
                rows = nn_dot(perm[pl.ds(0, BLK), :], cot[:, cols]) * scale
            stage[pl.ds(k, BLK, stride=SLAB), :] = rows
        pack(c, ZBLK)

    def dispatched(c):
        a2a_start(there, c)
        recv[c, z] = send[c, z]

    loads[0].wait()
    dispatch(0)
    pl.semaphore_wait(barrier, NZ + 4)

    w_copies = [
        remote(wg_hbm.at[0], wgu.at[pl.ds(FB, FB)], w_ssem.at[0], w_rsem.at[0], w_peer),
        remote(wu_hbm.at[0], wgu.at[pl.ds(3 * FB, FB)], w_ssem.at[1], w_rsem.at[1], w_peer),
        remote(wd_hbm.at[0], wd.at[pl.ds(FB, FB)], w_ssem.at[2], w_rsem.at[2], w_peer),
    ]
    for s in range(3):
        ahead_x(s).start()
    a2a_start(ahead_z, 0)
    recv[0, z, pl.ds(0, EBLK), :] = send[0, z, pl.ds(0, EBLK), :]
    for c in w_copies:
        c.start()
    for c in range(1, 4):
        if c == 2:
            loads[1].wait()
        dispatch(c)
        dispatched(c)

    for s in range(3):
        ahead_x(s).wait_recv()
        a2a_start(ahead_z, lands[s] + 1)
        over_x[0, lands[s], z] = ahead[lands[s], z]

    def by_x(c, s):
        return remote(
            halves(recv.at[c], min(s, 1)), over_x.at[c, lands[s]], p_ssem.at[c, s], p_rsem.at[c, lands[s]],
            x_peers[s],
        )

    def by_yx(c, s):
        f = Y_FIRST.index(c)
        return remote(
            halves(over_y.at[f], min(s, 1)), over_yx.at[f, lands[s]], q_ssem.at[f, s], q_rsem.at[f, lands[s]],
            x_peers[s],
        )

    def by_y(c):
        f = Y_FIRST.index(c)
        return remote(recv.at[c], over_y.at[f], h_ssem.at[f], h_rsem.at[f], y_peer)

    def by_xy(p):
        buf = (xa, ga)[p // NG]
        cols = pl.ds((p % NG) * GC, GC)
        return remote(
            buf.at[pl.ds(0, 2 * BLK), cols], buf.at[pl.ds(2 * BLK, 2 * BLK), cols],
            g_ssem.at[p], g_rsem.at[p], y_peer,
        )

    def unpack(c, first, own, others):
        buf = (xa, ga)[c // 2]

        def part(i):
            for s in range(4):
                r = pl.ds(pl.multiple_of((s * NZ + i) * EBLK, 16), EBLK)
                if s == 0:
                    stage[r, :] = own[i, pl.ds(0, EBLK), :].astype(F32)
                else:
                    stage[r, :] = others[s - 1, i].astype(F32)

        loop(NZ, part)
        for k in range(SLAB):
            cols = pl.ds((c % 2) * CH + k * LANES, LANES)
            buf[pl.ds(first, 2 * BLK), cols] = stage[pl.ds(k, 2 * BLK, stride=SLAB), :].astype(BF16)

    def onward(c):
        if c in Y_FIRST:
            by_y(c).wait_recv()
            for s in range(3):
                by_yx(c, s).start()
        else:
            for s in range(4):
                if c == 0:
                    a2a_arrived(ahead_z, s)
                elif s < 3:
                    by_x(c, s).wait_recv()
            unpack(c, 0, recv.at[c], over_x.at[c])
            for p in (2 * c, 2 * c + 1):
                by_xy(p).start()

    def settle(c):
        if c in Y_FIRST:
            f = Y_FIRST.index(c)
            for s in range(3):
                by_x(c, s).wait_recv()
            unpack(c, 0, recv.at[c], over_x.at[c])
            for s in range(3):
                by_yx(c, s).wait_recv()
            unpack(c, 2 * BLK, over_y.at[f], over_yx.at[f])
        else:
            for p in (2 * c, 2 * c + 1):
                by_xy(p).wait_recv()

    for c in range(1, 4):
        a2a_arrived(there, c)
        if c in Y_FIRST:
            by_y(c).start()
        for s in range(3):
            by_x(c, s).start()
        if c > 1:
            onward(c - 1)
    onward(0)
    onward(3)

    for c in loads[2:]:
        c.wait()
    for c in w_copies[:2]:
        c.wait_recv()

    def piece(p, w, acc):
        if p % 2 == 0:
            settle(p // 2)
        buf = (xa, ga)[p // NG]

        def part(k):
            cols = pl.ds(pl.multiple_of((p % NG) * GC + k * TC, TC), TC)
            t = nt_dot(buf[:, cols], w[:, cols])
            acc[...] = t + acc[...]

        loop(GC // TC, part)

    pre[...] = jnp.zeros_like(pre)
    hg[...] = jnp.zeros_like(hg)
    for p in range(NG):
        piece(p, wgu, pre)

    def activate(i):
        r = pl.ds(pl.multiple_of(i * 48, 16), 48)
        a = pre[r, 0 : 2 * FB]
        u = pre[r, 2 * FB : 4 * FB]
        sig = jax.nn.sigmoid(a)
        act = a * sig
        hid[r, :] = (act * u).astype(BF16)
        pre[r, 0 : 2 * FB] = u * (sig * (1.0 + a * (1.0 - sig)))
        pre[r, 2 * FB : 4 * FB] = act

    loop(ROWS // 48, activate)
    hidt = hid[...].T
    dt[2 * FB : 3 * FB, :] = hidt[FB : 2 * FB]
    dt[5 * FB : 6 * FB, :] = hidt[0:FB]

    w_copies[2].wait_recv()

    def e_sum(b):
        cols = pl.ds(pl.multiple_of(b * GC, GC), GC)
        rows = pl.ds(2 * FB, FB)
        return remote(dsend.at[rows, cols], drecv.at[rows, cols], e_ssem.at[b], e_rsem.at[b], w_peer)

    for p in range(NG, 2 * NG):
        piece(p, wd, hg)
        if p < 2 * NG - 1:
            cols = pl.ds((p % NG) * GC, GC)
            dsend[2 * FB : 3 * FB, cols] = nn_dot(dt[2 * FB : 3 * FB, :], ga[:, cols]).astype(BF16)
            if p - NG < EARLY_DOWN:
                e_sum(p - NG).start()
    for b in range(EARLY_DOWN, NG - 1):
        e_sum(b).start()

    def slopes(i):
        r = pl.ds(pl.multiple_of(i * 48, 16), 48)
        h = hg[r, :]
        gu[r, 0 : 2 * FB] = (h * pre[r, 0 : 2 * FB]).astype(BF16)
        gu[r, 2 * FB : 4 * FB] = (h * pre[r, 2 * FB : 4 * FB]).astype(BF16)

    loop(ROWS // 48, slopes)

    def tail_cols(j):
        return pl.ds(pl.multiple_of(j * TC, TC), TC)

    def outgoing(s):
        return wd.at[pl.ds(s * BLK, BLK)] if s < 2 else tx

    def x_sum(j, s):
        cols = tail_cols(j)
        return remote(
            outgoing(s).at[:, cols], rtx.at[lands[s], :, cols], x_ssem.at[j, s], x_rsem.at[j, lands[s]], x_peers[s]
        )

    def y_sum(j):
        cols = tail_cols(j)
        return remote(ty.at[:, cols], rty.at[:, cols], y_ssem.at[j], y_rsem.at[j], y_peer)

    def d_sum(j):
        cols = tail_cols(j)
        rows = pl.ds(0, 2 * FB)
        return remote(dsend.at[rows, cols], drecv.at[rows, cols], d_ssem.at[j], d_rsem.at[j], w_peer)

    def weights_out(j):
        cols = tail_cols(j)
        return [
            pltpu.make_async_copy(drecv.at[pl.ds(m * FB, FB), cols], o.at[0, :, cols], out_sem.at[m, j])
            for m, o in enumerate((og_hbm, ou_hbm, od_hbm))
        ]

    def other_weights(j):
        cols = tail_cols(j)
        dsend[0 : 2 * FB, cols] = nn_dot(dt[0 : 2 * FB, :], xa[:, cols]).astype(BF16)
        d_sum(j).start()

    def own_weights(j):
        cols = tail_cols(j)
        d_sum(j).wait_recv()
        a = nn_dot(dt[3 * FB : 5 * FB, :], xa[:, cols])
        drecv[0 : 2 * FB, cols] = (a + drecv[0 : 2 * FB, cols].astype(F32)).astype(BF16)
        @pl.when(j % 2 == 0)
        def _():
            e_sum(j // 2).wait_recv()

        b = nn_dot(dt[5 * FB : 6 * FB, :], ga[:, cols])
        drecv[2 * FB : 3 * FB, cols] = (b + drecv[2 * FB : 3 * FB, cols].astype(F32)).astype(BF16)
        for c in weights_out(j):
            c.start()

    def x_part(j):
        cols = tail_cols(j)
        t = nn_dot(gu[...], wgu[:, cols])

        def of(s):
            return jnp.concatenate(
                [t[s * HALF : (s + 1) * HALF], t[2 * BLK + s * HALF : 2 * BLK + (s + 1) * HALF]], axis=0
            ).astype(BF16)

        for s in range(3):
            outgoing(s)[:, cols] = of(s + 1)
            x_sum(j, s).start()
        kept[:, cols] = of(0)

    def sums(j, first):
        cols = tail_cols(j)
        a = kept[:, cols].astype(F32) + rtx[0, :, cols].astype(F32)
        b = rtx[1, :, cols].astype(F32) + rtx[2, :, cols].astype(F32)
        return jnp.concatenate([a[first : first + HALF], b[first : first + HALF]], axis=0)

    def y_part(j):
        for s in range(3):
            x_sum(j, s).wait_recv()
        ty[:, tail_cols(j)] = sums(j, HALF).astype(BF16)
        y_sum(j).start()

    for s in range(4):
        a2a_sent(ahead_z, s)
    for s in range(3):
        ahead_x(s).wait_send()
    for c in range(1, 4):
        a2a_sent(there, c)
        for s in range(3):
            by_x(c, s).wait_send()
        if c in Y_FIRST:
            by_y(c).wait_send()

    def own_part(j):
        y_sum(j).wait_recv()
        t = sums(j, 0) + rty[:, tail_cols(j)].astype(F32)
        t = nn_dot(order[:, 0:BLK], t.astype(BF16))
        for i in range(TC // LANES):
            stage[pl.ds((j % 2) * (TC // LANES) + i, BLK, stride=BSLAB), :] = t[:, i * LANES : (i + 1) * LANES]

        @pl.when(j % 2 == 1)
        def _():
            b = j // 2
            pack(b, BBLK)
            a2a_start(home, b)
            back[b, z] = send[b, z, pl.ds(0, BBLK), :]

    loop(HEAD, x_part)

    cols = pl.ds((NG - 1) * GC, GC)
    dsend[2 * FB : 3 * FB, cols] = nn_dot(dt[2 * FB : 3 * FB, :], ga[:, cols]).astype(BF16)
    e_sum(NG - 1).start()
    gut = gu[...].T
    dt[0:FB, :] = gut[FB : 2 * FB]
    dt[FB : 2 * FB, :] = gut[3 * FB : 4 * FB]
    dt[3 * FB : 4 * FB, :] = gut[0:FB]
    dt[4 * FB : 5 * FB, :] = gut[2 * FB : 3 * FB]
    loop(HEAD, other_weights)
    loop(NT, x_part, HEAD)
    loop(EARLY, other_weights, HEAD)

    def second(j):
        @pl.when(j < NT)
        def _():
            y_part(j)

        @pl.when(j + EARLY < NT)
        def _():
            other_weights(j + EARLY)

        @pl.when((j >= 1) & (j < NT + 1))
        def _():
            own_part(j - 1)

        @pl.when(j >= LAG)
        def _():
            own_weights(j - LAG)

    loop(NT + LAG, second)

    def tokens_out(b):
        cols = pl.ds(b * GC, GC)
        return pltpu.make_async_copy(tok.at[:, cols], tg_hbm.at[:, cols], tok_sem.at[b])

    for b in range(NG):
        a2a_arrived(home, b)

        def part(i, b=b):
            stage[pl.ds(pl.multiple_of(i * BBLK, 16), BBLK), :] = back[b, i].astype(F32)

        loop(NZ, part)
        for k in range(BSLAB):
            rows = stage[pl.ds(k, BLK, stride=BSLAB), :].astype(BF16)
            tok[:, pl.ds(b * GC + k * LANES, LANES)] = nn_dot(pt[:, 0:BLK], rows).astype(BF16)
        tokens_out(b).start()

    for c in w_copies:
        c.wait_send()
    for c in range(4):
        if c in Y_FIRST:
            for s in range(3):
                by_yx(c, s).wait_send()
        else:
            for p in (2 * c, 2 * c + 1):
                by_xy(p).wait_send()
    for b in range(NG):
        a2a_sent(home, b)
        e_sum(b).wait_send()

    def drain(j):
        for s in range(3):
            x_sum(j, s).wait_send()
        y_sum(j).wait_send()
        d_sum(j).wait_send()
        for c in weights_out(j):
            c.wait()

    loop(NT, drain)
    for b in range(NG):
        tokens_out(b).wait()


def copy_out(*refs):
    src, dst, held = refs[0:4], refs[4:8], refs[8:12]
    in_sem, out_sem = refs[12:]

    def parts(a, i):
        n = held[a].shape[0] // 4
        r = pl.ds(i * n, n)
        at = (r,) if a == 0 else (0, r)
        return (
            pltpu.make_async_copy(src[a].at[at], held[a].at[r], in_sem.at[a, i]),
            pltpu.make_async_copy(held[a].at[r], dst[a].at[at], out_sem.at[a, i]),
        )

    every = [parts(a, i) for a in range(4) for i in range(4)]
    for c, _ in every:
        c.start()
    for c, d in every:
        c.wait()
        d.start()
    for _, d in every:
        d.wait()


def local(tokens, cotangent, expert_ids, gate_weights, gate_proj, up_proj, down_proj):
    hbm = pl.BlockSpec(memory_space=pl.ANY)
    vmem = pl.BlockSpec(memory_space=pltpu.VMEM)
    dma = pltpu.SemaphoreType.DMA
    wide = jax.ShapeDtypeStruct((1, FB, D), BF16)
    outs = (jax.ShapeDtypeStruct((TOK, D), BF16), wide, wide, wide)
    done = pl.pallas_call(
        kernel,
        out_shape=outs,
        in_specs=[hbm, hbm, vmem, vmem, hbm, hbm, hbm],
        out_specs=(hbm, hbm, hbm, hbm),
        scratch_shapes=[
            pltpu.VMEM((TOK, D), BF16),
            pltpu.VMEM((TOK, D), BF16),
            pltpu.VMEM((TOK, 2 * LANES), BF16),
            pltpu.VMEM((2 * LANES, TOK), BF16),
            pltpu.VMEM((BLK, 2 * LANES), BF16),
            pltpu.VMEM((4 * FB, D), BF16),
            pltpu.VMEM((2 * FB, D), BF16),
            pltpu.VMEM((4, NZ, ZBLK, LANES), BF16),
            pltpu.VMEM((4, NZ, ZBLK, LANES), BF16),
            pltpu.VMEM((3, NZ, EBLK, LANES), BF16),
            pltpu.VMEM((len(Y_FIRST), NZ, ZBLK, LANES), BF16),
            pltpu.VMEM((4, 3, NZ, EBLK, LANES), BF16),
            pltpu.VMEM((len(Y_FIRST), 3, NZ, EBLK, LANES), BF16),
            pltpu.VMEM((4 * NZ * EBLK, LANES), F32),
            pltpu.VMEM((ROWS, D), BF16),
            pltpu.VMEM((ROWS, D), BF16),
            pltpu.VMEM((ROWS, 4 * FB), F32),
            pltpu.VMEM((ROWS, 2 * FB), F32),
            pltpu.VMEM((ROWS, 4 * FB), BF16),
            pltpu.VMEM((ROWS, 2 * FB), BF16),
            pltpu.VMEM((6 * FB, ROWS), BF16),
            pltpu.VMEM((BLK, D), BF16),
            pltpu.VMEM((3, BLK, D), BF16),
            pltpu.VMEM((BLK, D), BF16),
            pltpu.VMEM((BLK, D), BF16),
            pltpu.VMEM((BLK, D), BF16),
            pltpu.VMEM((3 * FB, D), BF16),
            pltpu.VMEM((3 * FB, D), BF16),
            pltpu.VMEM((NG, NZ, BBLK, LANES), BF16),
            dma((5,)),
            dma((3,)),
            dma((3,)),
            dma((4, NZ)),
            dma((4, NZ)),
            dma((4, NZ)),
            dma((4, NZ)),
            dma((4, 3)),
            dma((4, 3)),
            dma((len(Y_FIRST), 3)),
            dma((len(Y_FIRST), 3)),
            dma((2 * NG,)),
            dma((2 * NG,)),
            dma((len(Y_FIRST),)),
            dma((len(Y_FIRST),)),
            dma((NT, 3)),
            dma((NT, 3)),
            dma((NT,)),
            dma((NT,)),
            dma((NT,)),
            dma((NT,)),
            dma((NG,)),
            dma((NG,)),
            dma((NG, NZ)),
            dma((NG, NZ)),
            dma((3, NT)),
            dma((NG,)),
        ],
        cost_estimate=pl.CostEstimate(flops=14_500_000_000, bytes_accessed=12_500_000, transcendentals=300_000),
        compiler_params=pltpu.CompilerParams(
            collective_id=0, has_side_effects=True, vmem_limit_bytes=62 * 2**20
        ),
    )(
        tokens, cotangent, expert_ids.reshape(1, TOK), gate_weights.reshape(1, TOK),
        gate_proj, up_proj, down_proj,
    )
    return pl.pallas_call(
        copy_out,
        out_shape=outs,
        in_specs=[hbm] * 4,
        out_specs=(hbm,) * 4,
        scratch_shapes=[pltpu.VMEM((TOK, D), BF16)] + [pltpu.VMEM((FB, D), BF16)] * 3 + [dma((4, 4)), dma((4, 4))],
    )(*done)


def solution(mesh):
    rows = P(("group", "resp", "expert"), None)
    weights = P("expert", "resp", None)
    grads = P(("group", "expert"), "resp", None)
    return jax.shard_map(
        local,
        mesh=mesh,
        in_specs=(rows, rows, rows, rows, weights, weights, weights),
        out_specs=(rows, grads, grads, grads),
        check_vma=False,
    )
```

```python
import jax
import jax.numpy as jnp
from jax import lax
from jax.experimental import pallas as pl
from jax.experimental.pallas import tpu as pltpu
from jax.sharding import PartitionSpec as P

MESH = pl.DeviceIdType.MESH
BF16 = jnp.bfloat16
F32 = jnp.float32

TOK = 128
D = 4096
NE = 16
NZ = 8
CAP = 9
BLK = NE * CAP
HALF = NZ * CAP
FB = 192
ROWS = 4 * BLK
CH = 2048
LANES = 128
SLAB = CH // LANES
ZBLK = 2 * CAP * SLAB
EBLK = CAP * SLAB
GC = 1024
NG = D // GC
BSLAB = GC // LANES
BBLK = 2 * CAP * BSLAB
TC = 512
PART = 32
NT = D // TC
Y_FIRST = (1, 2)
EARLY_DOWN = 3
EARLY = 8
HEAD = 2
LAG = 3


def nt_dot(a, b):
    return lax.dot_general(a, b, (((1,), (1,)), ((), ())), preferred_element_type=F32)


def nn_dot(a, b):
    return jnp.dot(a, b, preferred_element_type=F32)


def loop(n, body, first=0):
    def step(i, carry):
        body(i)
        return carry

    lax.fori_loop(first, n, step, 0)


def kernel(
    tok_hbm, cot_hbm, ids_ref, gw_ref, wg_hbm, wu_hbm, wd_hbm,
    tg_hbm, og_hbm, ou_hbm, od_hbm,
    tok, cot, pt, perm, order, wgu, wd, send, recv, ahead, over_y, over_x, over_yx, stage, xa, ga,
    pre, hg, gu, hid, dt, tx, rtx, kept, ty, rty, dsend, drecv, back,
    load_sem, w_ssem, w_rsem, a_ssem, a_rsem, f_ssem, f_rsem, p_ssem, p_rsem, q_ssem, q_rsem, g_ssem, g_rsem, h_ssem, h_rsem,
    x_ssem, x_rsem, y_ssem, y_rsem, d_ssem, d_rsem, e_ssem, e_rsem, b_ssem, b_rsem,
    out_sem, tok_sem,
):
    resp = lax.axis_index("resp")
    expert = lax.axis_index("expert")
    core = lax.axis_index("group")
    y = resp // 2
    z = expert // 2
    x_lo = expert % 2
    x = (resp % 2) * 2 + x_lo
    side = (y + core) % 2

    def at(y, x, z):
        return {"resp": y * 2 + x // 2, "expert": z * 2 + x % 2}

    y_peer = at((y + 1 + 2 * side) % 4, x, z)
    w_peer = at((y + 3 + 2 * side) % 4, x, z)
    x_peers = [at(y, (x + d) % 4, z) for d in (2, 1, 3)]
    lands = (0, 2, 1)

    def remote(src, dst, ssem, rsem, to):
        return pltpu.make_async_remote_copy(
            src_ref=src, dst_ref=dst, send_sem=ssem, recv_sem=rsem, device_id=to, device_id_type=MESH
        )

    loads = [
        pltpu.make_async_copy(tok_hbm, tok, load_sem.at[0]),
        pltpu.make_async_copy(cot_hbm, cot, load_sem.at[1]),
        pltpu.make_async_copy(wg_hbm.at[0], wgu.at[pl.ds(0, FB)], load_sem.at[2]),
        pltpu.make_async_copy(wu_hbm.at[0], wgu.at[pl.ds(2 * FB, FB)], load_sem.at[3]),
        pltpu.make_async_copy(wd_hbm.at[0], wd.at[pl.ds(0, FB)], load_sem.at[4]),
    ]
    for c in loads:
        c.start()

    barrier = pltpu.get_barrier_semaphore()
    for peer in [y_peer, w_peer] + x_peers:
        pl.semaphore_signal(barrier, inc=1, device_id=peer, device_id_type=MESH)

    def greet(d):
        pl.semaphore_signal(barrier, inc=1, device_id=at(y, x, (z + d) % NZ), device_id_type=MESH)

    loop(NZ, greet, 1)

    ids = ids_ref[...]
    ids = ids + x_lo * (1 - 2 * (ids & 1))
    lane = lax.broadcasted_iota(jnp.int32, (TOK, TOK), 1)
    row = lax.broadcasted_iota(jnp.int32, (TOK, TOK), 0)
    onehot = jnp.where(row == ids, 1.0, 0.0).astype(F32)
    upper = jnp.where(row < lane, 1.0, 0.0).astype(BF16)
    rank = jnp.sum(nn_dot(onehot.astype(BF16), upper) * onehot, axis=0, keepdims=True).astype(jnp.int32)
    slot = lax.broadcasted_iota(jnp.int32, (2 * LANES, TOK), 0)
    chosen = jnp.where(slot == ids * CAP + rank, 1.0, 0.0).astype(F32)
    perm[...] = chosen.astype(BF16)
    pt[...] = chosen.T.astype(BF16)
    scale = jnp.sum(chosen * gw_ref[...], axis=1, keepdims=True)[0:BLK]
    to = lax.broadcasted_iota(jnp.int32, (BLK, 2 * LANES), 0)
    frm = lax.broadcasted_iota(jnp.int32, (BLK, 2 * LANES), 1)
    to_z = (to * 57) >> 10
    rest = to - to_z * (2 * CAP)
    rest = jnp.where(rest >= CAP, rest - CAP + HALF, rest)
    order[...] = jnp.where(frm == rest + to_z * CAP, 1.0, 0.0).astype(BF16)

    def there(c, other, mine):
        return remote(
            send.at[c, other], recv.at[c, mine], a_ssem.at[c, other], a_rsem.at[c, mine], at(y, x, other)
        )

    def home(c, other, mine):
        return remote(
            send.at[c, other, pl.ds(0, BBLK)], back.at[c, mine], b_ssem.at[c, other], b_rsem.at[c, mine],
            at(y, x, other),
        )

    def a2a_start(way, c):
        loop(NZ, lambda d: way(c, (z + d) % NZ, z).start(), 1)

    def a2a_arrived(way, c):
        def arrived(d):
            src = (z + d) % NZ
            way(c, src, src).wait_recv()

        loop(NZ, arrived, 1)

    def a2a_sent(way, c):
        loop(NZ, lambda d: way(c, (z + d) % NZ, z).wait_send(), 1)

    def halves(ref, i):
        return ref.at[:, pl.ds(i * EBLK, EBLK)]

    def ahead_x(s):
        return remote(
            halves(send.at[0], min(s, 1)), ahead.at[lands[s]], p_ssem.at[0, s], p_rsem.at[0, lands[s]], x_peers[s]
        )

    def ahead_z(s, other, mine):
        if s == 0:
            src, dst = send.at[0, other, pl.ds(0, EBLK)], recv.at[0, mine, pl.ds(0, EBLK)]
        else:
            src, dst = ahead.at[s - 1, other], over_x.at[0, s - 1, mine]
        return remote(src, dst, f_ssem.at[s, other], f_rsem.at[s, mine], at(y, x, other))

    def pack(c, rows):
        def part(i):
            send[c, i, pl.ds(0, rows), :] = stage[pl.ds(pl.multiple_of(i * rows, 16), rows), :].astype(BF16)

        loop(NZ, part)

    def dispatch(c):
        for k in range(SLAB):
            cols = pl.ds((c % 2) * CH + k * LANES, LANES)
            if c < 2:
                rows = nn_dot(perm[pl.ds(0, BLK), :], tok[:, cols])
            else:
                rows = nn_dot(perm[pl.ds(0, BLK), :], cot[:, cols]) * scale
            stage[pl.ds(k, BLK, stride=SLAB), :] = rows
        pack(c, ZBLK)

    def dispatched(c):
        a2a_start(there, c)
        recv[c, z] = send[c, z]

    loads[0].wait()
    dispatch(0)
    pl.semaphore_wait(barrier, NZ + 4)

    w_copies = [
        remote(wg_hbm.at[0], wgu.at[pl.ds(FB, FB)], w_ssem.at[0], w_rsem.at[0], w_peer),
        remote(wu_hbm.at[0], wgu.at[pl.ds(3 * FB, FB)], w_ssem.at[1], w_rsem.at[1], w_peer),
        remote(wd_hbm.at[0], wd.at[pl.ds(FB, FB)], w_ssem.at[2], w_rsem.at[2], w_peer),
    ]
    for s in range(3):
        ahead_x(s).start()
    a2a_start(ahead_z, 0)
    recv[0, z, pl.ds(0, EBLK), :] = send[0, z, pl.ds(0, EBLK), :]
    for c in w_copies:
        c.start()
    for c in range(1, 4):
        if c == 2:
            loads[1].wait()
        dispatch(c)
        dispatched(c)

    for s in range(3):
        ahead_x(s).wait_recv()
        a2a_start(ahead_z, lands[s] + 1)
        over_x[0, lands[s], z] = ahead[lands[s], z]

    def by_x(c, s):
        return remote(
            halves(recv.at[c], min(s, 1)), over_x.at[c, lands[s]], p_ssem.at[c, s], p_rsem.at[c, lands[s]],
            x_peers[s],
        )

    def by_yx(c, s):
        f = Y_FIRST.index(c)
        return remote(
            halves(over_y.at[f], min(s, 1)), over_yx.at[f, lands[s]], q_ssem.at[f, s], q_rsem.at[f, lands[s]],
            x_peers[s],
        )

    def by_y(c):
        f = Y_FIRST.index(c)
        return remote(recv.at[c], over_y.at[f], h_ssem.at[f], h_rsem.at[f], y_peer)

    def by_xy(p):
        buf = (xa, ga)[p // NG]
        cols = pl.ds((p % NG) * GC, GC)
        return remote(
            buf.at[pl.ds(0, 2 * BLK), cols], buf.at[pl.ds(2 * BLK, 2 * BLK), cols],
            g_ssem.at[p], g_rsem.at[p], y_peer,
        )

    def unpack(c, first, own, others):
        buf = (xa, ga)[c // 2]

        def part(i):
            for s in range(4):
                r = pl.ds(pl.multiple_of((s * NZ + i) * EBLK, 16), EBLK)
                if s == 0:
                    stage[r, :] = own[i, pl.ds(0, EBLK), :].astype(F32)
                else:
                    stage[r, :] = others[s - 1, i].astype(F32)

        loop(NZ, part)
        for k in range(SLAB):
            cols = pl.ds((c % 2) * CH + k * LANES, LANES)
            buf[pl.ds(first, 2 * BLK), cols] = stage[pl.ds(k, 2 * BLK, stride=SLAB), :].astype(BF16)

    def onward(c):
        if c in Y_FIRST:
            by_y(c).wait_recv()
            for s in range(3):
                by_yx(c, s).start()
        else:
            for s in range(4):
                if c == 0:
                    a2a_arrived(ahead_z, s)
                elif s < 3:
                    by_x(c, s).wait_recv()
            unpack(c, 0, recv.at[c], over_x.at[c])
            for p in (2 * c, 2 * c + 1):
                by_xy(p).start()

    def settle(c):
        if c in Y_FIRST:
            f = Y_FIRST.index(c)
            for s in range(3):
                by_x(c, s).wait_recv()
            unpack(c, 0, recv.at[c], over_x.at[c])
            for s in range(3):
                by_yx(c, s).wait_recv()
            unpack(c, 2 * BLK, over_y.at[f], over_yx.at[f])
        else:
            for p in (2 * c, 2 * c + 1):
                by_xy(p).wait_recv()

    for c in range(1, 4):
        a2a_arrived(there, c)
        if c in Y_FIRST:
            by_y(c).start()
        for s in range(3):
            by_x(c, s).start()
        if c > 1:
            onward(c - 1)
    onward(0)
    onward(3)

    for c in loads[2:]:
        c.wait()
    for c in w_copies[:2]:
        c.wait_recv()

    def piece(p, w, acc):
        if p % 2 == 0:
            settle(p // 2)
        buf = (xa, ga)[p // NG]

        def part(k):
            cols = pl.ds(pl.multiple_of((p % NG) * GC + k * TC, TC), TC)
            t = nt_dot(buf[:, cols], w[:, cols])
            acc[...] = t + acc[...]

        loop(GC // TC, part)

    pre[...] = jnp.zeros_like(pre)
    hg[...] = jnp.zeros_like(hg)
    for p in range(NG):
        piece(p, wgu, pre)

    def activate(i):
        r = pl.ds(pl.multiple_of(i * 48, 16), 48)
        a = pre[r, 0 : 2 * FB]
        u = pre[r, 2 * FB : 4 * FB]
        sig = jax.nn.sigmoid(a)
        act = a * sig
        hid[r, :] = (act * u).astype(BF16)
        pre[r, 0 : 2 * FB] = u * (sig * (1.0 + a * (1.0 - sig)))
        pre[r, 2 * FB : 4 * FB] = act

    loop(ROWS // 48, activate)
    hidt = hid[...].T
    dt[2 * FB : 3 * FB, :] = hidt[FB : 2 * FB]
    dt[5 * FB : 6 * FB, :] = hidt[0:FB]

    w_copies[2].wait_recv()

    def e_sum(b):
        cols = pl.ds(pl.multiple_of(b * GC, GC), GC)
        rows = pl.ds(2 * FB, FB)
        return remote(dsend.at[rows, cols], drecv.at[rows, cols], e_ssem.at[b], e_rsem.at[b], w_peer)

    for p in range(NG, 2 * NG):
        piece(p, wd, hg)
        if p < 2 * NG - 1:
            cols = pl.ds((p % NG) * GC, GC)
            dsend[2 * FB : 3 * FB, cols] = nn_dot(dt[2 * FB : 3 * FB, :], ga[:, cols]).astype(BF16)
            if p - NG < EARLY_DOWN:
                e_sum(p - NG).start()
    for b in range(EARLY_DOWN, NG - 1):
        e_sum(b).start()

    def slopes(i):
        r = pl.ds(pl.multiple_of(i * 48, 16), 48)
        h = hg[r, :]
        gu[r, 0 : 2 * FB] = (h * pre[r, 0 : 2 * FB]).astype(BF16)
        gu[r, 2 * FB : 4 * FB] = (h * pre[r, 2 * FB : 4 * FB]).astype(BF16)

    loop(ROWS // 48, slopes)

    def tail_cols(j):
        return pl.ds(pl.multiple_of(j * TC, TC), TC)

    def outgoing(s):
        return wd.at[pl.ds(s * BLK, BLK)] if s < 2 else tx

    def x_sum(j, s):
        cols = tail_cols(j)
        return remote(
            outgoing(s).at[:, cols], rtx.at[lands[s], :, cols], x_ssem.at[j, s], x_rsem.at[j, lands[s]], x_peers[s]
        )

    def y_sum(j):
        cols = tail_cols(j)
        return remote(ty.at[:, cols], rty.at[:, cols], y_ssem.at[j], y_rsem.at[j], y_peer)

    def d_sum(j):
        cols = tail_cols(j)
        rows = pl.ds(0, 2 * FB)
        return remote(dsend.at[rows, cols], drecv.at[rows, cols], d_ssem.at[j], d_rsem.at[j], w_peer)

    def weights_out(j):
        cols = tail_cols(j)
        return [
            pltpu.make_async_copy(drecv.at[pl.ds(m * FB, FB), cols], o.at[0, :, cols], out_sem.at[m, j])
            for m, o in enumerate((og_hbm, ou_hbm, od_hbm))
        ]

    def other_weights(j):
        cols = tail_cols(j)
        dsend[0 : 2 * FB, cols] = nn_dot(dt[0 : 2 * FB, :], xa[:, cols]).astype(BF16)
        d_sum(j).start()

    def own_weights(j):
        cols = tail_cols(j)
        d_sum(j).wait_recv()
        a = nn_dot(dt[3 * FB : 5 * FB, :], xa[:, cols])
        drecv[0 : 2 * FB, cols] = (a + drecv[0 : 2 * FB, cols].astype(F32)).astype(BF16)
        @pl.when(j % 2 == 0)
        def _():
            e_sum(j // 2).wait_recv()

        b = nn_dot(dt[5 * FB : 6 * FB, :], ga[:, cols])
        drecv[2 * FB : 3 * FB, cols] = (b + drecv[2 * FB : 3 * FB, cols].astype(F32)).astype(BF16)
        for c in weights_out(j):
            c.start()

    def x_part(j):
        cols = tail_cols(j)
        t = nn_dot(gu[...], wgu[:, cols])

        def of(s):
            return jnp.concatenate(
                [t[s * HALF : (s + 1) * HALF], t[2 * BLK + s * HALF : 2 * BLK + (s + 1) * HALF]], axis=0
            ).astype(BF16)

        for s in range(3):
            outgoing(s)[:, cols] = of(s + 1)
            x_sum(j, s).start()
        kept[:, cols] = of(0)

    def sums(j, first):
        cols = tail_cols(j)
        a = kept[:, cols].astype(F32) + rtx[0, :, cols].astype(F32)
        b = rtx[1, :, cols].astype(F32) + rtx[2, :, cols].astype(F32)
        return jnp.concatenate([a[first : first + HALF], b[first : first + HALF]], axis=0)

    def y_part(j):
        for s in range(3):
            x_sum(j, s).wait_recv()
        ty[:, tail_cols(j)] = sums(j, HALF).astype(BF16)
        y_sum(j).start()

    for s in range(4):
        a2a_sent(ahead_z, s)
    for s in range(3):
        ahead_x(s).wait_send()
    for c in range(1, 4):
        a2a_sent(there, c)
        for s in range(3):
            by_x(c, s).wait_send()
        if c in Y_FIRST:
            by_y(c).wait_send()

    def own_part(j):
        y_sum(j).wait_recv()
        t = sums(j, 0) + rty[:, tail_cols(j)].astype(F32)
        t = nn_dot(order[:, 0:BLK], t.astype(BF16))
        for i in range(TC // LANES):
            stage[pl.ds((j % 2) * (TC // LANES) + i, BLK, stride=BSLAB), :] = t[:, i * LANES : (i + 1) * LANES]

        @pl.when(j % 2 == 1)
        def _():
            b = j // 2
            pack(b, BBLK)
            a2a_start(home, b)
            back[b, z] = send[b, z, pl.ds(0, BBLK), :]

    loop(HEAD, x_part)

    cols = pl.ds((NG - 1) * GC, GC)
    dsend[2 * FB : 3 * FB, cols] = nn_dot(dt[2 * FB : 3 * FB, :], ga[:, cols]).astype(BF16)
    e_sum(NG - 1).start()
    gut = gu[...].T
    dt[0:FB, :] = gut[FB : 2 * FB]
    dt[FB : 2 * FB, :] = gut[3 * FB : 4 * FB]
    dt[3 * FB : 4 * FB, :] = gut[0:FB]
    dt[4 * FB : 5 * FB, :] = gut[2 * FB : 3 * FB]
    loop(HEAD, other_weights)
    loop(NT, x_part, HEAD)
    loop(EARLY, other_weights, HEAD)

    def second(j):
        @pl.when(j < NT)
        def _():
            y_part(j)

        @pl.when(j + EARLY < NT)
        def _():
            other_weights(j + EARLY)

        @pl.when((j >= 1) & (j < NT + 1))
        def _():
            own_part(j - 1)

        @pl.when(j >= LAG)
        def _():
            own_weights(j - LAG)

    loop(NT + LAG, second)

    def tokens_out(b):
        cols = pl.ds(b * GC, GC)
        return pltpu.make_async_copy(tok.at[:, cols], tg_hbm.at[:, cols], tok_sem.at[b])

    for b in range(NG):
        a2a_arrived(home, b)

        def part(i, b=b):
            stage[pl.ds(pl.multiple_of(i * BBLK, 16), BBLK), :] = back[b, i].astype(F32)

        loop(NZ, part)
        for k in range(BSLAB):
            rows = stage[pl.ds(k, BLK, stride=BSLAB), :].astype(BF16)
            tok[:, pl.ds(b * GC + k * LANES, LANES)] = nn_dot(pt[:, 0:BLK], rows).astype(BF16)
        tokens_out(b).start()

    for c in w_copies:
        c.wait_send()
    for c in range(4):
        if c in Y_FIRST:
            for s in range(3):
                by_yx(c, s).wait_send()
        else:
            for p in (2 * c, 2 * c + 1):
                by_xy(p).wait_send()
    for b in range(NG):
        a2a_sent(home, b)
        e_sum(b).wait_send()

    def drain(j):
        for s in range(3):
            x_sum(j, s).wait_send()
        y_sum(j).wait_send()
        d_sum(j).wait_send()
        for c in weights_out(j):
            c.wait()

    loop(NT, drain)
    for b in range(NG):
        tokens_out(b).wait()


def copy_out(*refs):
    src, dst, held = refs[0:4], refs[4:8], refs[8:12]
    in_sem, out_sem = refs[12:]

    def parts(a, i):
        r = pl.ds(i * PART, PART)
        at = (r,) if a == 0 else (0, r)
        return (
            pltpu.make_async_copy(src[a].at[at], held[a].at[r], in_sem.at[a, i]),
            pltpu.make_async_copy(held[a].at[r], dst[a].at[at], out_sem.at[a, i]),
        )

    every = [parts(a, i) for a in range(4) for i in range(held[a].shape[0] // PART)]
    for c, _ in every:
        c.start()
    for c, d in every:
        c.wait()
        d.start()
    for _, d in every:
        d.wait()


def local(tokens, cotangent, expert_ids, gate_weights, gate_proj, up_proj, down_proj):
    hbm = pl.BlockSpec(memory_space=pl.ANY)
    vmem = pl.BlockSpec(memory_space=pltpu.VMEM)
    dma = pltpu.SemaphoreType.DMA
    wide = jax.ShapeDtypeStruct((1, FB, D), BF16)
    outs = (jax.ShapeDtypeStruct((TOK, D), BF16), wide, wide, wide)
    done = pl.pallas_call(
        kernel,
        out_shape=outs,
        in_specs=[hbm, hbm, vmem, vmem, hbm, hbm, hbm],
        out_specs=(hbm, hbm, hbm, hbm),
        scratch_shapes=[
            pltpu.VMEM((TOK, D), BF16),
            pltpu.VMEM((TOK, D), BF16),
            pltpu.VMEM((TOK, 2 * LANES), BF16),
            pltpu.VMEM((2 * LANES, TOK), BF16),
            pltpu.VMEM((BLK, 2 * LANES), BF16),
            pltpu.VMEM((4 * FB, D), BF16),
            pltpu.VMEM((2 * FB, D), BF16),
            pltpu.VMEM((4, NZ, ZBLK, LANES), BF16),
            pltpu.VMEM((4, NZ, ZBLK, LANES), BF16),
            pltpu.VMEM((3, NZ, EBLK, LANES), BF16),
            pltpu.VMEM((len(Y_FIRST), NZ, ZBLK, LANES), BF16),
            pltpu.VMEM((4, 3, NZ, EBLK, LANES), BF16),
            pltpu.VMEM((len(Y_FIRST), 3, NZ, EBLK, LANES), BF16),
            pltpu.VMEM((4 * NZ * EBLK, LANES), F32),
            pltpu.VMEM((ROWS, D), BF16),
            pltpu.VMEM((ROWS, D), BF16),
            pltpu.VMEM((ROWS, 4 * FB), F32),
            pltpu.VMEM((ROWS, 2 * FB), F32),
            pltpu.VMEM((ROWS, 4 * FB), BF16),
            pltpu.VMEM((ROWS, 2 * FB), BF16),
            pltpu.VMEM((6 * FB, ROWS), BF16),
            pltpu.VMEM((BLK, D), BF16),
            pltpu.VMEM((3, BLK, D), BF16),
            pltpu.VMEM((BLK, D), BF16),
            pltpu.VMEM((BLK, D), BF16),
            pltpu.VMEM((BLK, D), BF16),
            pltpu.VMEM((3 * FB, D), BF16),
            pltpu.VMEM((3 * FB, D), BF16),
            pltpu.VMEM((NG, NZ, BBLK, LANES), BF16),
            dma((5,)),
            dma((3,)),
            dma((3,)),
            dma((4, NZ)),
            dma((4, NZ)),
            dma((4, NZ)),
            dma((4, NZ)),
            dma((4, 3)),
            dma((4, 3)),
            dma((len(Y_FIRST), 3)),
            dma((len(Y_FIRST), 3)),
            dma((2 * NG,)),
            dma((2 * NG,)),
            dma((len(Y_FIRST),)),
            dma((len(Y_FIRST),)),
            dma((NT, 3)),
            dma((NT, 3)),
            dma((NT,)),
            dma((NT,)),
            dma((NT,)),
            dma((NT,)),
            dma((NG,)),
            dma((NG,)),
            dma((NG, NZ)),
            dma((NG, NZ)),
            dma((3, NT)),
            dma((NG,)),
        ],
        cost_estimate=pl.CostEstimate(flops=14_500_000_000, bytes_accessed=12_500_000, transcendentals=300_000),
        compiler_params=pltpu.CompilerParams(
            collective_id=0, has_side_effects=True, vmem_limit_bytes=62 * 2**20
        ),
    )(
        tokens, cotangent, expert_ids.reshape(1, TOK), gate_weights.reshape(1, TOK),
        gate_proj, up_proj, down_proj,
    )
    return pl.pallas_call(
        copy_out,
        out_shape=outs,
        in_specs=[hbm] * 4,
        out_specs=(hbm,) * 4,
        scratch_shapes=[pltpu.VMEM((TOK, D), BF16)] + [pltpu.VMEM((FB, D), BF16)] * 3 + [dma((4, FB // PART))] * 2,
    )(*done)


def solution(mesh):
    rows = P(("group", "resp", "expert"), None)
    weights = P("expert", "resp", None)
    grads = P(("group", "expert"), "resp", None)
    return jax.shard_map(
        local,
        mesh=mesh,
        in_specs=(rows, rows, rows, rows, weights, weights, weights),
        out_specs=(rows, grads, grads, grads),
        check_vma=False,
    )
```
